128 devices in a mesh: grp: 4 (over x_lo, core), dom: 32 (over y, x_hi, z).
Axes of the slice: x: 4 (x_hi: 2, x_lo: 2; x = x_hi * 2 + x_lo), y: 4, z: 4, core: 2. Of those that a mesh axis runs over, the one named last changes fastest.
Arguments:
- state: float32 [8192, 4, 72, 128], P(('grp', 'dom')), may hold values from -6 to 6
- neighbours: int32 [8192, 4], P(('grp', 'dom')), may hold values from 0 to 67, as said below
- remap_dest: int32 [65536], P(('grp', 'dom')), may hold values from 0 to 127, as said below
- remap_src: int32 [65536], P(('grp', 'dom')), may hold values from 0 to 63
- remap_block: int32 [65536], P(('grp', 'dom')), may hold values from 0 to 63
- remap_weights: float32 [65536, 128], P(('grp', 'dom')), may hold values from 0.2 to 1
- self_op: float32 [2, 128, 128], replicated, may hold values from -0.5 to 0.5
- edge_op: float32 [2, 128, 128], replicated, may hold values from -0.25 to 0.25
- vert_op: float32 [2, 72, 72], replicated, may hold values from -0.75 to 0.75
Outputs:
- new_state: float32 [8192, 4, 72, 128], P(('grp', 'dom'))
The draws below stay inside these ranges and needn't reach their ends.
Inputs may be any that keep to these rules, and one draw needn't show every extreme that they name: Value v of local block b names local block v - 2 of the same device if 0 <= v - 2 < 64, else a block of the previous or next device along dom (wrapping); v lies between b and b + 4. The first two neighbours are the blocks b - 1 and b + 1. `remap_dest`: flat device index over grp and dom (grp slowest). Rows of an atmosphere device go to ocean devices, exactly 16 to each; rows of an ocean device go to atmosphere devices, exactly 16 to the atmosphere devices of each dom index together, at most 16 to any, exactly 16 to one.
All inputs are finite; a program needn't handle non-finite values.
Results may differ from the reference program's by a relative error of at most 0.0001.
Values sent between devices are 32-bit elements; how exact they have to be, the bound alone decides.
A program may use at most 192 MiB of HBM per device.

```python
import jax
import jax.numpy as jnp
from jax import lax

COLS = 128
LEV = 72
FIELDS = 4
NBRS = 4
H = 2
SUBSTEPS = 2
B = 64
CAP = 16
OVL = 512
N_GRP = 4
N_DOM = 32
DEVICES = 128


def draw_neighbours(key, part):
    key = jax.random.fold_in(key, 11)
    rows = N_GRP * N_DOM * B
    local = jnp.arange(rows, dtype=jnp.int32) % B
    spare = local[:, None] + jax.random.randint(key, (rows, 2), 0, 2 * H + 1)
    left = local - 1 + H
    right = local + 1 + H
    third = jnp.where(local == 0, 0, spare[:, 0])
    fourth = jnp.where(local == B - 1, B + 2 * H - 1, spare[:, 1])
    return jnp.stack([left, right, third, fourth], axis=1).astype(jnp.int32)


def draw_remap_dest(key, part):
    key = jax.random.fold_in(key, 23)
    devices = N_GRP * N_DOM
    count = CAP * N_DOM
    key_pick, key_group, key_fixed, key_order = jax.random.split(key, 4)
    group = jnp.arange(count, dtype=jnp.int32) // CAP
    toward_ocean = (N_GRP - 1) * N_DOM + group
    picks = jax.random.randint(key_pick, (devices, count), 0, N_GRP - 1)
    forced_group = jax.random.randint(key_group, (devices, 1), 0, N_DOM)
    forced_pick = jax.random.randint(key_fixed, (devices, 1), 0, N_GRP - 1)
    picks = jnp.where(group[None, :] == forced_group, forced_pick, picks)
    toward_atmos = picks * N_DOM + group[None, :]
    is_ocean = jnp.arange(devices, dtype=jnp.int32) >= (N_GRP - 1) * N_DOM
    dest = jnp.where(is_ocean[:, None], toward_atmos, toward_ocean[None, :])
    order_keys = jax.random.split(key_order, devices)
    orders = jax.vmap(lambda single: jax.random.permutation(single, count))(order_keys)
    dest = jnp.take_along_axis(dest, orders, axis=1)
    return dest.reshape(-1).astype(jnp.int32)


def touch_ends(entries, stream_key, low, top_value):
    longest = entries.shape.index(max(entries.shape))
    spots = []
    for shift in (0, 1):
        where = [jax.random.randint(jax.random.fold_in(stream_key, axis), (), 0, length) for axis, length in enumerate(entries.shape)]
        where[longest] = (where[longest] + shift) % entries.shape[longest]
        spots.append(tuple(where))
    return entries.at[spots[0]].set(low).at[spots[1]].set(top_value)


def levels(own_key, extent, shards, least, largest):
    gain = 1.0
    for dim, shards_of in shards:
        steps = jax.random.uniform(jax.random.fold_in(jax.random.fold_in(own_key, 6), dim), (shards_of,), jnp.float32, least / len(shards), largest / len(shards))
        gain = gain * jnp.repeat(jnp.exp(steps), extent[dim] // shards_of).reshape((-1,) + (1,) * (len(extent) - 1 - dim))
    return gain


def gaussian(rng, dims, width, bound, cuts=(), held_as=jnp.bfloat16):
    level = levels(rng, dims, cuts, -0.22, 0.18) if cuts else 1.0
    result = jax.random.normal(rng, dims, jnp.float32) * width * level
    return jnp.minimum(jnp.maximum(result, -bound), bound).astype(held_as)


def setup_inputs(seed: int = 0) -> dict:
    keys = jax.random.split(jax.random.key(seed), 10)
    state = gaussian(keys[0], (DEVICES * B, FIELDS, LEV, COLS), 1.0, 6.0, ((0, 128),), jnp.float32)
    neighbours = draw_neighbours(jax.random.fold_in(keys[9], 71), 0)
    remap_dest = draw_remap_dest(jax.random.fold_in(keys[9], 71), 0)
    remap_src = touch_ends(jax.random.randint(keys[3], (DEVICES * OVL,), 0, B), jax.random.fold_in(keys[3], 1), 0, B - 1).astype(jnp.int32)
    remap_block = touch_ends(jax.random.randint(keys[4], (DEVICES * OVL,), 0, B), jax.random.fold_in(keys[4], 1), 0, B - 1).astype(jnp.int32)
    remap_weights = jnp.clip(0.2 + 0.8 * jax.random.uniform(keys[5], (DEVICES * OVL, COLS), jnp.float32) ** levels(keys[5], (DEVICES * OVL, COLS), ((0, 128),), -0.2, 0.2), 0.2, 1.0)
    self_op = gaussian(keys[6], (2, COLS, COLS), COLS ** -0.5, 0.5, (), jnp.float32)
    edge_op = gaussian(keys[7], (2, COLS, COLS), (NBRS * COLS) ** -0.5, 0.25, (), jnp.float32)
    vert_op = gaussian(keys[8], (2, LEV, LEV), LEV ** -0.5, 0.75, (), jnp.float32)
    return {"state": state, "neighbours": neighbours, "remap_dest": remap_dest, "remap_src": remap_src, "remap_block": remap_block, "remap_weights": remap_weights, "self_op": self_op, "edge_op": edge_op, "vert_op": vert_op}


def advance(field, cycle_index, self_m, edge_m, vert_m):
    nbrsum = field[cycle_index[:, 0]]
    for slot in range(1, NBRS):
        nbrsum = nbrsum + field[cycle_index[:, slot]]
    lateral = field + 0.5 * (jnp.matmul(field, self_m, precision=lax.Precision.HIGHEST) + jnp.matmul(nbrsum, edge_m, precision=lax.Precision.HIGHEST))
    return jnp.einsum('lm,bfmc->bflc', vert_m, lateral, precision=lax.Precision.HIGHEST)


def reference(state, neighbours, remap_dest, remap_src, remap_block, remap_weights, self_op, edge_op, vert_op):
    devices = N_GRP * N_DOM
    cycle = N_DOM * B
    grid = state.reshape(N_GRP, cycle, FIELDS, LEV, COLS)
    nbr = neighbours.reshape(N_GRP, N_DOM, B, NBRS).astype(jnp.int32)
    home = (jnp.arange(N_DOM, dtype=jnp.int32) * B)[:, None, None]
    cycle_index = ((home + nbr - H) % cycle).astype(jnp.int32).reshape(N_GRP, cycle, NBRS)
    stepped_list = []
    for group in range(N_GRP):
        comp = 1 if group == N_GRP - 1 else 0
        field = grid[group]
        for sub in range(SUBSTEPS):
            field = advance(field, cycle_index[group], self_op[comp], edge_op[comp], vert_op[comp])
        stepped_list.append(field)
    stepped = jnp.stack(stepped_list).reshape(devices * B, FIELDS, LEV, COLS)
    rows = remap_dest.shape[0]
    sender = (jnp.arange(rows, dtype=jnp.int32) // OVL).astype(jnp.int32)
    send_level = jnp.where(sender // N_DOM == N_GRP - 1, 0, LEV - 1).astype(jnp.int32)
    flat_zero = state[:, 0]
    source = (sender * B + remap_src).astype(jnp.int32)
    values = remap_weights * flat_zero[source, send_level]
    target = (remap_dest * B + remap_block).astype(jnp.int32)
    received = jax.ops.segment_sum(values, target, num_segments=devices * B)
    owner = (jnp.arange(devices * B, dtype=jnp.int32) // B).astype(jnp.int32)
    dest_level = jnp.where(owner // N_DOM == N_GRP - 1, 0, LEV - 1).astype(jnp.int32)
    level_mask = (jnp.arange(LEV, dtype=jnp.int32)[None, :] == dest_level[:, None]).astype(state.dtype)
    return stepped.at[:, 0].add(level_mask[:, :, None] * received[:, None, :])
```

```python
import functools

import jax
import jax.numpy as jnp
from jax import lax
from jax.experimental import pallas as pl
from jax.experimental.pallas import tpu as pltpu
from jax.sharding import PartitionSpec as P

MESH = pl.DeviceIdType.MESH
F32 = jnp.float32
BF16 = jnp.bfloat16
NZ = 4
CAP = 16
RIM = 4
RELAY = 1
ROWS = NZ * CAP
MSG = ROWS + 8
CHUNKS = 4


def split(v):
    hi = v.astype(BF16)
    return hi, (v - hi.astype(F32)).astype(BF16)


def dot(a, b):
    return jnp.dot(a, b, preferred_element_type=F32)


def dot_nt(a, b):
    return lax.dot_general(a, b, (((1,), (1,)), ((), ())), preferred_element_type=F32)


def exact(a, b):
    return jnp.dot(a, b, precision=lax.Precision.HIGHEST, preferred_element_type=F32)


def pick(onehot, v):
    hi, lo = split(v)
    both = dot(onehot, jnp.concatenate([hi, lo], axis=1))
    width = v.shape[1]
    return both[:, :width] + both[:, width:]


def iota(shape, dim):
    return lax.broadcasted_iota(jnp.int32, shape, dim)


def kernel(
    n_grp, n_dom,
    state, nbr_in, dest_in, src_in, blk_in, wts_in, self_in, edge_in, vert_in,
    out,
    xv, nx, hl, hr, nbr, dest, src, blk, wts, selfv, edgev, vertv,
    wa, wc, vcat, mo, ml, mr, sb, rb, fb, fid, db, ob, gb, tot,
    sem_x, sem_in, sem_halo_s, sem_halo_r, sem_m_s, sem_m_r,
    sem_p1_s, sem_p1_r, sem_p2_s, sem_p2_r, sem_p3_s, sem_p3_r,
):
    blocks, fields, lev, cols = state.shape
    n_gi = n_dom // NZ
    lanes = n_gi * CAP
    ocean_g = n_grp - 1
    g = lax.axis_index("grp")
    d = lax.axis_index("dom")
    gi = d // NZ
    z = lax.rem(d, NZ)
    is_ocean = g == ocean_g
    is_relay = g == RELAY
    comp = jnp.where(is_ocean, 1, 0)
    right = (g, lax.rem(d + 1, n_dom))
    left = (g, lax.rem(d + n_dom - 1, n_dom))

    per = blocks // CHUNKS
    loads_x = [
        pltpu.make_async_copy(
            state.at[pl.ds(i * per, per)], xv.at[pl.ds(i * per, per)], sem_x.at[i]
        )
        for i in range(CHUNKS)
    ]
    pairs = [
        (nbr_in, nbr), (dest_in, dest), (src_in, src), (blk_in, blk), (wts_in, wts),
        (self_in.at[comp], selfv), (edge_in.at[comp], edgev), (vert_in.at[comp], vertv),
    ]
    loads = [pltpu.make_async_copy(a, b, sem_in.at[i]) for i, (a, b) in enumerate(pairs)]
    for c in loads:
        c.start()
    for c in loads_x:
        c.start()

    barrier = pltpu.get_barrier_semaphore()

    def greet(gg, dd):
        pl.semaphore_signal(barrier, inc=1, device_id=(gg, dd), device_id_type=MESH)

    greet(*left)
    greet(*right)

    @pl.when(is_ocean)
    def _():
        for q in range(n_gi):
            for gg in range(ocean_g):
                greet(gg, q * NZ + z)
        for r in range(1, NZ):
            greet(ocean_g, gi * NZ + lax.rem(z + r, NZ))

    @pl.when(jnp.logical_not(is_ocean))
    def _():
        for q in range(n_gi):
            greet(ocean_g, q * NZ + z)

    @pl.when(is_relay)
    def _():
        for r in range(1, NZ):
            greet(RELAY, gi * NZ + lax.rem(z + r, NZ))
        for gg in range(ocean_g):
            if gg != RELAY:
                greet(gg, d)

    @pl.when(jnp.logical_not(jnp.logical_or(is_relay, is_ocean)))
    def _():
        greet(RELAY, d)

    greetings = jnp.where(
        is_ocean,
        2 + n_gi * ocean_g + NZ - 1,
        jnp.where(is_relay, 2 + n_gi + NZ - 1 + ocean_g - 1, 2 + n_gi + 1),
    )
    pl.semaphore_wait(barrier, greetings)

    halo = []
    for f in range(fields):
        halo.append(
            pltpu.make_async_remote_copy(
                src_ref=state.at[pl.ds(blocks - RIM, RIM), f], dst_ref=hl.at[f],
                send_sem=sem_halo_s.at[0, f], recv_sem=sem_halo_r.at[0, f],
                device_id=right, device_id_type=MESH,
            )
        )
        halo.append(
            pltpu.make_async_remote_copy(
                src_ref=state.at[pl.ds(0, RIM), f], dst_ref=hr.at[f],
                send_sem=sem_halo_s.at[1, f], recv_sem=sem_halo_r.at[1, f],
                device_id=left, device_id_type=MESH,
            )
        )
    for c in halo:
        c.start()

    loads[0].wait()
    mo[...] = jnp.zeros_like(mo)
    for side in range(2):
        for k in range(2):
            b = k if side == 0 else blocks - 2 + k
            third = nbr[b, 2]
            fourth = nbr[b, 3]
            for j in range(5):
                count = jnp.where(third == b + j, 1.0, 0.0) + jnp.where(fourth == b + j, 1.0, 0.0)
                row = side * 16 + k * 5 + j
                mo[row : row + 1, :] = jnp.full((1, cols), count, F32)
    counts = [
        pltpu.make_async_remote_copy(
            src_ref=mo.at[pl.ds(16, 16)], dst_ref=ml, send_sem=sem_m_s.at[0],
            recv_sem=sem_m_r.at[0], device_id=right, device_id_type=MESH,
        ),
        pltpu.make_async_remote_copy(
            src_ref=mo.at[pl.ds(0, 16)], dst_ref=mr, send_sem=sem_m_s.at[1],
            recv_sem=sem_m_r.at[1], device_id=left, device_id_type=MESH,
        ),
    ]
    for c in counts:
        c.start()

    for c in loads[1:5]:
        c.wait()
    n_rows = n_dom * CAP
    key = lax.rem(dest[...], n_dom)
    code = blk[...] + jnp.where(is_ocean, blocks, 0) * (dest[...] // n_dom)
    toward = (iota((n_dom, n_rows), 0) == key).astype(BF16)
    before = (iota((n_rows, n_rows), 0) < iota((n_rows, n_rows), 1)).astype(BF16)
    rank = jnp.sum(toward.astype(F32) * dot(toward, before), axis=0, keepdims=True)
    slot = key.astype(F32) * CAP + rank
    perm = (iota((n_rows, n_rows), 0).astype(F32) == slot).astype(BF16)
    weights = pick(perm, wts[...])
    origin = (iota((blocks, n_rows), 0) == src[...]).astype(BF16)
    origin = dot_nt(perm, origin).astype(BF16)
    lane = (gi * CAP).astype(F32) + rank
    at_lane = (iota((cols, n_rows), 0).astype(F32) == lane).astype(BF16)
    key8 = (key // NZ) * 8 + lax.rem(key, NZ)
    coded = jnp.where(iota((n_gi * 8, n_rows), 0) == key8, code.astype(F32), 0.0).astype(BF16)
    targets = dot_nt(coded, at_lane)
    for c in loads_x:
        c.wait()
    surface = jnp.where(is_ocean, xv[:, 0, 0, :], xv[:, 0, lev - 1, :])
    values = weights * pick(origin, surface)
    sb[:, 0:ROWS, :] = values.reshape(n_gi, ROWS, cols)
    sb[:, ROWS:MSG, :] = targets.reshape(n_gi, 8, cols)
    to_grp = jnp.where(is_ocean, RELAY, ocean_g)
    my_slot = jnp.where(is_ocean, gi, g * n_gi + gi)
    first = [
        pltpu.make_async_remote_copy(
            src_ref=sb.at[q], dst_ref=rb.at[my_slot], send_sem=sem_p1_s.at[q],
            recv_sem=sem_p1_r.at[my_slot], device_id=(to_grp, q * NZ + z), device_id_type=MESH,
        )
        for q in range(n_gi)
    ]
    for c in first:
        c.start()

    for c in loads[5:]:
        c.wait()
    eye = (iota((cols, cols), 0) == iota((cols, cols), 1)).astype(F32)
    a = eye + 0.5 * selfv[...]
    e = 0.5 * edgev[...]
    a2h, a2l = split(exact(a, a))
    ch, cl = split(exact(e, a) + exact(a, e))
    e2h, e2l = split(exact(e, e))
    wa[0:cols, 0:cols] = a2h
    wa[0:cols, cols : 2 * cols] = a2l
    wa[cols : 2 * cols, 0:cols] = ch
    wa[cols : 2 * cols, cols : 2 * cols] = cl
    for half in range(2):
        wc[half * cols : (half + 1) * cols, 0:cols] = e2h
        wc[half * cols : (half + 1) * cols, cols : 2 * cols] = e2l
    v2 = exact(vertv[...], vertv[...])
    v2h = v2.astype(BF16).astype(F32)
    vcat[...] = jnp.concatenate([v2h, v2h, v2 - v2h], axis=1).astype(BF16)

    def lateral(x, n1, n2):
        xh, xl = split(x)
        n1h, n1l = split(n1)
        n2h, n2l = split(n2)
        p = dot(jnp.concatenate([xh, n1h], axis=1), wa[...])
        p += dot(jnp.concatenate([xl, n1l], axis=1), wa[...])
        p += dot(jnp.concatenate([n2h, n2l], axis=1), wc[...])
        return p[:, 0:cols] + p[:, cols:]

    def vertical(v):
        hi = v.astype(BF16).astype(F32)
        return dot(vcat[...], jnp.concatenate([hi, v - hi, hi], axis=0).astype(BF16))

    def near(b):
        third_ = jnp.clip(nbr[b, 2] - 2, 0, blocks - 1)
        fourth_ = jnp.clip(nbr[b, 3] - 2, 0, blocks - 1)
        return xv[b - 1] + xv[b + 1] + xv[third_] + xv[fourth_]

    def inner(b, carry):
        x = xv[b].reshape(fields * lev, cols)
        n1 = nx[b + 2].reshape(fields * lev, cols)
        n2 = (nx[b + 1] + nx[b + 3] + nx[nbr[b, 2]] + nx[nbr[b, 3]]).reshape(fields * lev, cols)
        lat = lateral(x, n1, n2)
        for f in range(0, fields, 2):
            pair = jnp.concatenate(
                [lat[f * lev : (f + 1) * lev], lat[(f + 1) * lev : (f + 2) * lev]], axis=1
            )
            res = vertical(pair)
            out[b, f] = res[:, 0:cols]
            out[b, f + 1] = res[:, cols:]
        later = jnp.minimum(b + 3, blocks - 3)
        nx[later + 2] = near(later)
        return carry

    for b in range(2, 7):
        nx[b + 2] = near(b)
    span = blocks - 2 * RIM
    cuts = [RIM, RIM + span // 3, RIM + 2 * span // 3, blocks - RIM]
    lax.fori_loop(cuts[0], cuts[1], inner, 0)

    def received_wait(dst, sem):
        pltpu.make_async_remote_copy(
            src_ref=dst, dst_ref=dst, send_sem=sem, recv_sem=sem,
            device_id=left, device_id_type=MESH,
        ).wait_recv()

    def dense(rows, ids, height):
        return pick((iota((height, lanes), 0) == ids).astype(BF16), rows)

    def second(make):
        return [make(r, gi * NZ + lax.rem(z + r, NZ)) for r in range(1, NZ)]

    def ocean_copy(r, dd):
        return pltpu.make_async_remote_copy(
            src_ref=db.at[lax.rem(z + r, NZ)], dst_ref=ob.at[z], send_sem=sem_p2_s.at[r, 0],
            recv_sem=sem_p2_r.at[z, 0], device_id=(ocean_g, dd), device_id_type=MESH,
        )

    def relay_rows(r, dd):
        zz = lax.rem(z + r, NZ)
        return pltpu.make_async_remote_copy(
            src_ref=rb.at[pl.ds(0, n_gi), pl.ds(pl.multiple_of(zz * CAP, CAP), CAP)],
            dst_ref=fb.at[z], send_sem=sem_p2_s.at[r, 0],
            recv_sem=sem_p2_r.at[z, 0], device_id=(RELAY, dd), device_id_type=MESH,
        )

    def relay_ids(r, dd):
        return pltpu.make_async_remote_copy(
            src_ref=rb.at[pl.ds(0, n_gi), pl.ds(ROWS, 8)],
            dst_ref=fid.at[z], send_sem=sem_p2_s.at[r, 1],
            recv_sem=sem_p2_r.at[z, 1], device_id=(RELAY, dd), device_id_type=MESH,
        )

    @pl.when(is_ocean)
    def _():
        for s in range(ocean_g * n_gi):
            received_wait(rb.at[s], sem_p1_r.at[s])
        for zz in range(NZ):
            total = jnp.zeros((blocks, cols), F32)
            for gg in range(ocean_g):
                sl = slice(gg * n_gi, (gg + 1) * n_gi)
                rows = rb[sl, zz * CAP : (zz + 1) * CAP, :].reshape(lanes, cols)
                ids = jnp.sum(rb[sl, ROWS:MSG, :], axis=0)[zz : zz + 1, 0:lanes].astype(jnp.int32)
                total += dense(rows, ids, blocks)
            db[zz] = total
        for c in second(ocean_copy):
            c.start()

    @pl.when(is_relay)
    def _():
        for s in range(n_gi):
            received_wait(rb.at[s], sem_p1_r.at[s])
        for c in second(relay_rows) + second(relay_ids):
            c.start()

    lax.fori_loop(cuts[1], cuts[2], inner, 0)

    def third(gg, slot_):
        return pltpu.make_async_remote_copy(
            src_ref=tot.at[pl.ds(gg * blocks, blocks)], dst_ref=gb,
            send_sem=sem_p3_s.at[slot_], recv_sem=sem_p3_r.at[0],
            device_id=(gg, d), device_id_type=MESH,
        )

    def thirds():
        others = [gg for gg in range(ocean_g) if gg != RELAY]
        return [third(gg, i) for i, gg in enumerate(others)]

    @pl.when(is_relay)
    def _():
        own_rows = rb[0:n_gi, pl.ds(pl.multiple_of(z * CAP, CAP), CAP), :]
        own_ids = rb[0:n_gi, ROWS:MSG, :]

        def add(rows, ids8):
            mine = jnp.where(iota((8, cols), 0) == z, jnp.sum(ids8, axis=0), 0.0)
            ids = jnp.sum(mine, axis=0, keepdims=True)[:, 0:lanes].astype(jnp.int32)
            return dense(rows.reshape(lanes, cols), ids, ocean_g * blocks)

        tot[...] = add(own_rows, own_ids)
        for r in range(1, NZ):
            zz = lax.rem(z + r, NZ)
            received_wait(fb.at[zz], sem_p2_r.at[zz, 0])
            received_wait(fid.at[zz], sem_p2_r.at[zz, 1])
            tot[...] += add(fb[zz], fid[zz])
        for c in thirds():
            c.start()

    lax.fori_loop(cuts[2], cuts[3], inner, 0)

    for c in counts:
        c.wait_recv()
    for f in range(fields):
        halo[2 * f].wait_recv()
        halo[2 * f + 1].wait_recv()
        for side in range(2):
            base = 0 if side == 0 else blocks - RIM

            def at(k):
                if side == 0:
                    return hl[f, k] if k < RIM else xv[k - RIM, f]
                return xv[blocks - RIM + k, f] if k < RIM else hr[f, k - RIM]

            for k in range(2, 6):
                outer = k < 4 if side == 0 else k >= 4
                if side == 0:
                    m, row = (ml, (k - 2) * 5) if outer else (mo, (k - 4) * 5)
                else:
                    m, row = (mr, (k - 4) * 5) if outer else (mo, 16 + (k - 2) * 5)
                acc = at(k - 1) + at(k + 1)
                for j in range(5):
                    acc += m[row + j : row + j + 1, :] * at(k - 2 + j)
                at_row = k - 2 if side == 0 else blocks - 2 + k
                nx[at_row, f] = acc
            xs, n1s, n2s = [], [], []
            for k in range(RIM):
                b = base + k
                xs.append(xv[b, f])
                n1s.append(nx[b + 2, f])
                n2s.append(nx[b + 1, f] + nx[b + 3, f] + nx[nbr[b, 2], f] + nx[nbr[b, 3], f])
            lat = lateral(*(jnp.concatenate(v, axis=0) for v in (xs, n1s, n2s)))
            for k in range(0, RIM, 2):
                pair = jnp.concatenate(
                    [lat[k * lev : (k + 1) * lev], lat[(k + 1) * lev : (k + 2) * lev]], axis=1
                )
                res = vertical(pair)
                out[base + k, f] = res[:, 0:cols]
                out[base + k + 1, f] = res[:, cols:]

    @pl.when(is_ocean)
    def _():
        got = db[z]
        for r in range(1, NZ):
            zz = lax.rem(z + r, NZ)
            received_wait(ob.at[zz], sem_p2_r.at[zz, 0])
            got += ob[zz]
        out[:, 0, 0, :] += got
        for c in second(ocean_copy):
            c.wait_send()

    @pl.when(is_relay)
    def _():
        out[:, 0, lev - 1, :] += tot[RELAY * blocks : (RELAY + 1) * blocks, :]
        for c in second(relay_rows) + second(relay_ids) + thirds():
            c.wait_send()

    @pl.when(jnp.logical_not(jnp.logical_or(is_relay, is_ocean)))
    def _():
        received_wait(gb, sem_p3_r.at[0])
        out[:, 0, lev - 1, :] += gb[...]

    for c in halo + counts + first:
        c.wait_send()


def per_device(
    state, neighbours, remap_dest, remap_src, remap_block, remap_weights, self_op, edge_op, vert_op
):
    n_grp = lax.axis_size("grp")
    n_dom = lax.axis_size("dom")
    blocks, fields, lev, cols = state.shape
    n_rows = remap_dest.shape[0]
    n_gi = n_dom // NZ
    dma = pltpu.SemaphoreType.DMA
    vm = pltpu.VMEM
    call = pl.pallas_call(
        functools.partial(kernel, n_grp, n_dom),
        out_shape=pltpu.VMEM(state.shape, F32),
        in_specs=[pl.BlockSpec(memory_space=pl.ANY)] * 9,
        out_specs=pl.BlockSpec(memory_space=pltpu.VMEM),
        scratch_shapes=[
            vm(state.shape, F32),
            vm((blocks + 4, fields, lev, cols), F32),
            vm((fields, RIM, lev, cols), F32),
            vm((fields, RIM, lev, cols), F32),
            pltpu.SMEM(neighbours.shape, jnp.int32),
            vm((1, n_rows), jnp.int32),
            vm((1, n_rows), jnp.int32),
            vm((1, n_rows), jnp.int32),
            vm((n_rows, cols), F32),
            vm((cols, cols), F32),
            vm((cols, cols), F32),
            vm((lev, lev), F32),
            vm((2 * cols, 2 * cols), BF16),
            vm((2 * cols, 2 * cols), BF16),
            vm((lev, 3 * lev), BF16),
            vm((32, cols), F32),
            vm((16, cols), F32),
            vm((16, cols), F32),
            vm((n_gi, MSG, cols), F32),
            vm(((n_grp - 1) * n_gi, MSG, cols), F32),
            vm((NZ, n_gi, CAP, cols), F32),
            vm((NZ, n_gi, 8, cols), F32),
            vm((NZ, blocks, cols), F32),
            vm((NZ, blocks, cols), F32),
            vm((blocks, cols), F32),
            vm(((n_grp - 1) * blocks, cols), F32),
            dma((CHUNKS,)),
            dma((8,)),
            dma((2, fields)),
            dma((2, fields)),
            dma((2,)),
            dma((2,)),
            dma((n_gi,)),
            dma(((n_grp - 1) * n_gi,)),
            dma((NZ, 2)),
            dma((NZ, 2)),
            dma((n_grp - 2,)),
            dma((1,)),
        ],
        compiler_params=pltpu.CompilerParams(
            collective_id=0, has_side_effects=True, vmem_limit_bytes=46 * 1024 * 1024
        ),
        name="interval",
    )
    return call(
        state,
        neighbours,
        remap_dest.reshape(1, n_rows),
        remap_src.reshape(1, n_rows),
        remap_block.reshape(1, n_rows),
        remap_weights,
        self_op,
        edge_op,
        vert_op,
    )


def solution(mesh):
    in_specs = (
        P(("grp", "dom"), None, None, None),
        P(("grp", "dom"), None),
        P(("grp", "dom")),
        P(("grp", "dom")),
        P(("grp", "dom")),
        P(("grp", "dom"), None),
        P(),
        P(),
        P(),
    )
    out_specs = P(("grp", "dom"), None, None, None)
    return jax.shard_map(
        per_device, mesh=mesh, in_specs=in_specs, out_specs=out_specs, check_vma=False
    )
```

```python
import functools

import jax
import jax.numpy as jnp
from jax import lax
from jax.experimental import pallas as pl
from jax.experimental.pallas import tpu as pltpu
from jax.sharding import PartitionSpec as P

MESH = pl.DeviceIdType.MESH
F32 = jnp.float32
BF16 = jnp.bfloat16
NZ = 4
CAP = 16
RIM = 4
RELAY = 1
ROWS = NZ * CAP
MSG = ROWS + 8
CHUNKS = 4
UNIT = 8
SECOND, THIRD = 5, 7


def split(v):
    hi = v.astype(BF16)
    return hi, (v - hi.astype(F32)).astype(BF16)


def dot(a, b):
    return jnp.dot(a, b, preferred_element_type=F32)


def dot_nt(a, b):
    return lax.dot_general(a, b, (((1,), (1,)), ((), ())), preferred_element_type=F32)


def exact(a, b):
    return jnp.dot(a, b, precision=lax.Precision.HIGHEST, preferred_element_type=F32)


def pick(onehot, v):
    hi, lo = split(v)
    both = dot(onehot, jnp.concatenate([hi, lo], axis=1))
    width = v.shape[1]
    return both[:, :width] + both[:, width:]


def iota(shape, dim):
    return lax.broadcasted_iota(jnp.int32, shape, dim)


def kernel(
    n_grp, n_dom,
    state, nbr_in, dest_in, src_in, blk_in, wts_in, self_in, edge_in, vert_in,
    out,
    xv, nx, hl, hr, nbr, dest, src, blk, wts, selfv, edgev, vertv,
    wa, wc, vcat, mo, ml, mr, sb, rb, fb, fid, db, ob, gb, tot,
    sem_x, sem_in, sem_halo_s, sem_halo_r, sem_m_s, sem_m_r,
    sem_p1_s, sem_p1_r, sem_p2_s, sem_p2_r, sem_p3_s, sem_p3_r,
):
    blocks, fields, lev, cols = state.shape
    n_gi = n_dom // NZ
    lanes = n_gi * CAP
    ocean_g = n_grp - 1
    g = lax.axis_index("grp")
    d = lax.axis_index("dom")
    gi = d // NZ
    z = lax.rem(d, NZ)
    is_ocean = g == ocean_g
    is_relay = g == RELAY
    comp = jnp.where(is_ocean, 1, 0)
    right = (g, lax.rem(d + 1, n_dom))
    left = (g, lax.rem(d + n_dom - 1, n_dom))

    per = blocks // CHUNKS
    loads_x = [
        pltpu.make_async_copy(
            state.at[pl.ds(i * per, per)], xv.at[pl.ds(i * per, per)], sem_x.at[i]
        )
        for i in range(CHUNKS)
    ]
    pairs = [
        (nbr_in, nbr), (dest_in, dest), (src_in, src), (blk_in, blk), (wts_in, wts),
        (self_in.at[comp], selfv), (edge_in.at[comp], edgev), (vert_in.at[comp], vertv),
    ]
    loads = [pltpu.make_async_copy(a, b, sem_in.at[i]) for i, (a, b) in enumerate(pairs)]
    for c in loads:
        c.start()
    for c in loads_x:
        c.start()

    barrier = pltpu.get_barrier_semaphore()

    def greet(gg, dd):
        pl.semaphore_signal(barrier, inc=1, device_id=(gg, dd), device_id_type=MESH)

    greet(*left)
    greet(*right)

    @pl.when(is_ocean)
    def _():
        for q in range(n_gi):
            for gg in range(ocean_g):
                greet(gg, q * NZ + z)
        for r in range(1, NZ):
            greet(ocean_g, gi * NZ + lax.rem(z + r, NZ))

    @pl.when(jnp.logical_not(is_ocean))
    def _():
        for q in range(n_gi):
            greet(ocean_g, q * NZ + z)

    @pl.when(is_relay)
    def _():
        for r in range(1, NZ):
            greet(RELAY, gi * NZ + lax.rem(z + r, NZ))
        for gg in range(ocean_g):
            if gg != RELAY:
                greet(gg, d)

    @pl.when(jnp.logical_not(jnp.logical_or(is_relay, is_ocean)))
    def _():
        greet(RELAY, d)

    greetings = jnp.where(
        is_ocean,
        2 + n_gi * ocean_g + NZ - 1,
        jnp.where(is_relay, 2 + n_gi + NZ - 1 + ocean_g - 1, 2 + n_gi + 1),
    )
    halo = []
    for f in range(fields):
        halo.append(
            pltpu.make_async_remote_copy(
                src_ref=state.at[pl.ds(blocks - RIM, RIM), f], dst_ref=hl.at[f],
                send_sem=sem_halo_s.at[0, f], recv_sem=sem_halo_r.at[0, f],
                device_id=right, device_id_type=MESH,
            )
        )
        halo.append(
            pltpu.make_async_remote_copy(
                src_ref=state.at[pl.ds(0, RIM), f], dst_ref=hr.at[f],
                send_sem=sem_halo_s.at[1, f], recv_sem=sem_halo_r.at[1, f],
                device_id=left, device_id_type=MESH,
            )
        )
    loads[0].wait()
    mo[...] = jnp.zeros_like(mo)
    for side in range(2):
        for k in range(2):
            b = k if side == 0 else blocks - 2 + k
            third = nbr[2, b]
            fourth = nbr[3, b]
            for j in range(5):
                count = jnp.where(third == b + j, 1.0, 0.0) + jnp.where(fourth == b + j, 1.0, 0.0)
                row = side * 16 + k * 5 + j
                mo[row : row + 1, :] = jnp.full((1, cols), count, F32)
    counts = [
        pltpu.make_async_remote_copy(
            src_ref=mo.at[pl.ds(16, 16)], dst_ref=ml, send_sem=sem_m_s.at[0],
            recv_sem=sem_m_r.at[0], device_id=right, device_id_type=MESH,
        ),
        pltpu.make_async_remote_copy(
            src_ref=mo.at[pl.ds(0, 16)], dst_ref=mr, send_sem=sem_m_s.at[1],
            recv_sem=sem_m_r.at[1], device_id=left, device_id_type=MESH,
        ),
    ]
    for c in loads[1:5]:
        c.wait()
    n_rows = n_dom * CAP
    key = lax.rem(dest[...], n_dom)
    code = blk[...] + jnp.where(is_ocean, blocks, 0) * (dest[...] // n_dom)
    toward = (iota((n_dom, n_rows), 0) == key).astype(BF16)
    before = (iota((n_rows, n_rows), 0) < iota((n_rows, n_rows), 1)).astype(BF16)
    rank = jnp.sum(toward.astype(F32) * dot(toward, before), axis=0, keepdims=True)
    slot = key.astype(F32) * CAP + rank
    perm = (iota((n_rows, n_rows), 0).astype(F32) == slot).astype(BF16)
    weights = pick(perm, wts[...])
    origin = (iota((blocks, n_rows), 0) == src[...]).astype(BF16)
    origin = dot_nt(perm, origin).astype(BF16)
    lane = (gi * CAP).astype(F32) + rank
    at_lane = (iota((cols, n_rows), 0).astype(F32) == lane).astype(BF16)
    key8 = (key // NZ) * 8 + lax.rem(key, NZ)
    coded = jnp.where(iota((n_gi * 8, n_rows), 0) == key8, code.astype(F32), 0.0).astype(BF16)
    targets = dot_nt(coded, at_lane)
    for c in loads_x:
        c.wait()
    surface = jnp.where(is_ocean, xv[:, 0, 0, :], xv[:, 0, lev - 1, :])
    values = weights * pick(origin, surface)
    sb[:, 0:ROWS, :] = values.reshape(n_gi, ROWS, cols)
    sb[:, ROWS:MSG, :] = targets.reshape(n_gi, 8, cols)
    to_grp = jnp.where(is_ocean, RELAY, ocean_g)
    my_slot = jnp.where(is_ocean, gi, g * n_gi + gi)
    first = [
        pltpu.make_async_remote_copy(
            src_ref=sb.at[q], dst_ref=rb.at[my_slot], send_sem=sem_p1_s.at[q],
            recv_sem=sem_p1_r.at[my_slot], device_id=(to_grp, q * NZ + z), device_id_type=MESH,
        )
        for q in range(n_gi)
    ]
    for c in loads[5:]:
        c.wait()
    eye = (iota((cols, cols), 0) == iota((cols, cols), 1)).astype(F32)
    a = eye + 0.5 * selfv[...]
    e = 0.5 * edgev[...]
    a2h, a2l = split(exact(a, a))
    ch, cl = split(exact(e, a) + exact(a, e))
    e2h, e2l = split(exact(e, e))
    wa[0:cols, 0:cols] = a2h
    wa[0:cols, cols : 2 * cols] = a2l
    wa[cols : 2 * cols, 0:cols] = ch
    wa[cols : 2 * cols, cols : 2 * cols] = cl
    for half in range(2):
        wc[half * cols : (half + 1) * cols, 0:cols] = e2h
        wc[half * cols : (half + 1) * cols, cols : 2 * cols] = e2l
    v2 = exact(vertv[...], vertv[...])
    v2h = v2.astype(BF16).astype(F32)
    vcat[...] = jnp.concatenate([v2h, v2h, v2 - v2h], axis=1).astype(BF16)

    def lateral(x, n1, n2):
        xh, xl = split(x)
        n1h, n1l = split(n1)
        n2h, n2l = split(n2)
        p = dot(jnp.concatenate([xh, n1h], axis=1), wa[...])
        p += dot(jnp.concatenate([xl, n1l], axis=1), wa[...])
        p += dot(jnp.concatenate([n2h, n2l], axis=1), wc[...])
        return p[:, 0:cols] + p[:, cols:]

    def vertical(v):
        hi = v.astype(BF16).astype(F32)
        return dot(vcat[...], jnp.concatenate([hi, v - hi, hi], axis=0).astype(BF16))

    def near(b):
        third_ = jnp.clip(nbr[2, b] - 2, 0, blocks - 1)
        fourth_ = jnp.clip(nbr[3, b] - 2, 0, blocks - 1)
        return xv[b - 1] + xv[b + 1] + xv[third_] + xv[fourth_]

    for b in range(2, RIM + UNIT + 2):
        nx[b + 2] = near(b)

    pl.semaphore_wait(barrier, greetings)
    for c in halo + counts + first:
        c.start()

    def received_wait(dst, sem):
        pltpu.make_async_remote_copy(
            src_ref=dst, dst_ref=dst, send_sem=sem, recv_sem=sem,
            device_id=left, device_id_type=MESH,
        ).wait_recv()

    def dense(rows, ids, height):
        return pick((iota((height, lanes), 0) == ids).astype(BF16), rows)

    def second(make):
        return [make(r, gi * NZ + lax.rem(z + r, NZ)) for r in range(1, NZ)]

    def ocean_copy(r, dd):
        return pltpu.make_async_remote_copy(
            src_ref=db.at[lax.rem(z + r, NZ)], dst_ref=ob.at[z], send_sem=sem_p2_s.at[r, 0],
            recv_sem=sem_p2_r.at[z, 0], device_id=(ocean_g, dd), device_id_type=MESH,
        )

    def relay_rows(r, dd):
        zz = lax.rem(z + r, NZ)
        return pltpu.make_async_remote_copy(
            src_ref=rb.at[pl.ds(0, n_gi), pl.ds(pl.multiple_of(zz * CAP, CAP), CAP)],
            dst_ref=fb.at[z], send_sem=sem_p2_s.at[r, 0],
            recv_sem=sem_p2_r.at[z, 0], device_id=(RELAY, dd), device_id_type=MESH,
        )

    def relay_ids(r, dd):
        return pltpu.make_async_remote_copy(
            src_ref=rb.at[pl.ds(0, n_gi), pl.ds(ROWS, 8)],
            dst_ref=fid.at[z], send_sem=sem_p2_s.at[r, 1],
            recv_sem=sem_p2_r.at[z, 1], device_id=(RELAY, dd), device_id_type=MESH,
        )

    def ocean_second():
        for s in range(ocean_g * n_gi):
            received_wait(rb.at[s], sem_p1_r.at[s])
        for zz in range(NZ):
            total = jnp.zeros((blocks, cols), F32)
            for gg in range(ocean_g):
                sl = slice(gg * n_gi, (gg + 1) * n_gi)
                rows = rb[sl, zz * CAP : (zz + 1) * CAP, :].reshape(lanes, cols)
                ids = jnp.sum(rb[sl, ROWS:MSG, :], axis=0)[zz : zz + 1, 0:lanes].astype(jnp.int32)
                total += dense(rows, ids, blocks)
            db[zz] = total
        for c in second(ocean_copy):
            c.start()

    def relay_second():
        for s in range(n_gi):
            received_wait(rb.at[s], sem_p1_r.at[s])
        for c in second(relay_rows) + second(relay_ids):
            c.start()

    def third(gg, slot_):
        return pltpu.make_async_remote_copy(
            src_ref=tot.at[pl.ds(gg * blocks, blocks)], dst_ref=gb,
            send_sem=sem_p3_s.at[slot_], recv_sem=sem_p3_r.at[0],
            device_id=(gg, d), device_id_type=MESH,
        )

    def thirds():
        others = [gg for gg in range(ocean_g) if gg != RELAY]
        return [third(gg, i) for i, gg in enumerate(others)]

    def relay_third():
        own_rows = rb[0:n_gi, pl.ds(pl.multiple_of(z * CAP, CAP), CAP), :]
        own_ids = rb[0:n_gi, ROWS:MSG, :]

        def add(rows, ids8):
            mine = jnp.where(iota((8, cols), 0) == z, jnp.sum(ids8, axis=0), 0.0)
            ids = jnp.sum(mine, axis=0, keepdims=True)[:, 0:lanes].astype(jnp.int32)
            return dense(rows.reshape(lanes, cols), ids, ocean_g * blocks)

        tot[...] = add(own_rows, own_ids)
        for r in range(1, NZ):
            zz = lax.rem(z + r, NZ)
            received_wait(fb.at[zz], sem_p2_r.at[zz, 0])
            received_wait(fid.at[zz], sem_p2_r.at[zz, 1])
            tot[...] += add(fb[zz], fid[zz])
        for c in thirds():
            c.start()

    def outer_sums():
        for c in counts + halo:
            c.wait_recv()
        for side in range(2):

            def at(k):
                if side == 0:
                    return hl[:, k] if k < RIM else xv[k - RIM]
                return xv[blocks - RIM + k] if k < RIM else hr[:, k - RIM]

            for k in range(2, 6):
                if side == 0:
                    m, row = (ml, (k - 2) * 5) if k < 4 else (mo, (k - 4) * 5)
                else:
                    m, row = (mr, (k - 4) * 5) if k >= 4 else (mo, 16 + (k - 2) * 5)
                acc = at(k - 1) + at(k + 1)
                for j in range(5):
                    acc += m[row + j : row + j + 1, :] * at(k - 2 + j)
                nx[k - 2 if side == 0 else blocks - 2 + k] = acc

    def step(i, carry):
        pl.when(jnp.logical_and(is_ocean, i == SECOND))(ocean_second)
        pl.when(jnp.logical_and(is_relay, i == SECOND))(relay_second)
        pl.when(jnp.logical_and(is_relay, i == THIRD))(relay_third)
        pl.when(i == steps - 1)(outer_sums)
        mine = [lax.rem(RIM + i * UNIT + u, blocks) for u in range(UNIT)]
        high = fields * lev
        xs = [xv[b].reshape(high, cols) for b in mine]
        n1s = [nx[b + 2].reshape(high, cols) for b in mine]
        n2s = [
            (nx[b + 1] + nx[b + 3] + nx[nbr[2, b]] + nx[nbr[3, b]]).reshape(high, cols)
            for b in mine
        ]
        lat = lateral(*(jnp.concatenate(v, axis=0) for v in (xs, n1s, n2s)))
        for u, b in enumerate(mine):
            for f in range(0, fields, 2):
                o = u * high + f * lev
                pair = jnp.concatenate([lat[o : o + lev], lat[o + lev : o + 2 * lev]], axis=1)
                res = vertical(pair)
                out[b, f] = res[:, 0:cols]
                out[b, f + 1] = res[:, cols:]
        for u in range(UNIT):
            later = jnp.minimum(RIM + (i + 1) * UNIT + 2 + u, blocks - 3)
            nx[later + 2] = near(later)
        return carry

    steps = blocks // UNIT
    lax.fori_loop(0, steps, step, 0)

    @pl.when(is_ocean)
    def _():
        got = db[z]
        for r in range(1, NZ):
            zz = lax.rem(z + r, NZ)
            received_wait(ob.at[zz], sem_p2_r.at[zz, 0])
            got += ob[zz]
        out[:, 0, 0, :] += got
        for c in second(ocean_copy):
            c.wait_send()

    @pl.when(is_relay)
    def _():
        out[:, 0, lev - 1, :] += tot[RELAY * blocks : (RELAY + 1) * blocks, :]
        for c in second(relay_rows) + second(relay_ids) + thirds():
            c.wait_send()

    @pl.when(jnp.logical_not(jnp.logical_or(is_relay, is_ocean)))
    def _():
        received_wait(gb, sem_p3_r.at[0])
        out[:, 0, lev - 1, :] += gb[...]

    for c in halo + counts + first:
        c.wait_send()


def per_device(
    state, neighbours, remap_dest, remap_src, remap_block, remap_weights, self_op, edge_op, vert_op
):
    n_grp = lax.axis_size("grp")
    n_dom = lax.axis_size("dom")
    blocks, fields, lev, cols = state.shape
    n_rows = remap_dest.shape[0]
    n_gi = n_dom // NZ
    dma = pltpu.SemaphoreType.DMA
    vm = pltpu.VMEM
    call = pl.pallas_call(
        functools.partial(kernel, n_grp, n_dom),
        out_shape=pltpu.VMEM(state.shape, F32),
        in_specs=[pl.BlockSpec(memory_space=pl.ANY)] * 9,
        out_specs=pl.BlockSpec(memory_space=pltpu.VMEM),
        scratch_shapes=[
            vm(state.shape, F32),
            vm((blocks + 4, fields, lev, cols), F32),
            vm((fields, RIM, lev, cols), F32),
            vm((fields, RIM, lev, cols), F32),
            pltpu.SMEM(neighbours.shape[::-1], jnp.int32),
            vm((1, n_rows), jnp.int32),
            vm((1, n_rows), jnp.int32),
            vm((1, n_rows), jnp.int32),
            vm((n_rows, cols), F32),
            vm((cols, cols), F32),
            vm((cols, cols), F32),
            vm((lev, lev), F32),
            vm((2 * cols, 2 * cols), BF16),
            vm((2 * cols, 2 * cols), BF16),
            vm((lev, 3 * lev), BF16),
            vm((32, cols), F32),
            vm((16, cols), F32),
            vm((16, cols), F32),
            vm((n_gi, MSG, cols), F32),
            vm(((n_grp - 1) * n_gi, MSG, cols), F32),
            vm((NZ, n_gi, CAP, cols), F32),
            vm((NZ, n_gi, 8, cols), F32),
            vm((NZ, blocks, cols), F32),
            vm((NZ, blocks, cols), F32),
            vm((blocks, cols), F32),
            vm(((n_grp - 1) * blocks, cols), F32),
            dma((CHUNKS,)),
            dma((8,)),
            dma((2, fields)),
            dma((2, fields)),
            dma((2,)),
            dma((2,)),
            dma((n_gi,)),
            dma(((n_grp - 1) * n_gi,)),
            dma((NZ, 2)),
            dma((NZ, 2)),
            dma((n_grp - 2,)),
            dma((1,)),
        ],
        compiler_params=pltpu.CompilerParams(
            collective_id=0, has_side_effects=True, vmem_limit_bytes=46 * 1024 * 1024
        ),
        name="interval",
    )
    return call(
        state,
        neighbours.T,
        remap_dest.reshape(1, n_rows),
        remap_src.reshape(1, n_rows),
        remap_block.reshape(1, n_rows),
        remap_weights,
        self_op,
        edge_op,
        vert_op,
    )


def solution(mesh):
    in_specs = (
        P(("grp", "dom"), None, None, None),
        P(("grp", "dom"), None),
        P(("grp", "dom")),
        P(("grp", "dom")),
        P(("grp", "dom")),
        P(("grp", "dom"), None),
        P(),
        P(),
        P(),
    )
    out_specs = P(("grp", "dom"), None, None, None)
    return jax.shard_map(
        per_device, mesh=mesh, in_specs=in_specs, out_specs=out_specs, check_vma=False
    )
```

```python
import functools

import jax
import jax.numpy as jnp
from jax import lax
from jax.experimental import pallas as pl
from jax.experimental.pallas import tpu as pltpu
from jax.sharding import PartitionSpec as P

MESH = pl.DeviceIdType.MESH
F32 = jnp.float32
BF16 = jnp.bfloat16
NZ = 4
CAP = 16
RIM = 4
RELAY = 1
ROWS = NZ * CAP
MSG = ROWS + 8
CHUNKS = 4
UNIT = 8
SECOND = 6
EARLY = 6


def split(v):
    hi = v.astype(BF16)
    return hi, (v - hi.astype(F32)).astype(BF16)


def dot(a, b):
    return jnp.dot(a, b, preferred_element_type=F32)


def dot_nt(a, b):
    return lax.dot_general(a, b, (((1,), (1,)), ((), ())), preferred_element_type=F32)


def exact(a, b):
    return jnp.dot(a, b, precision=lax.Precision.HIGHEST, preferred_element_type=F32)


def pick(onehot, v):
    hi, lo = split(v)
    both = dot(onehot, jnp.concatenate([hi, lo], axis=1))
    width = v.shape[1]
    return both[:, :width] + both[:, width:]


def iota(shape, dim):
    return lax.broadcasted_iota(jnp.int32, shape, dim)


def kernel(
    n_grp, n_dom,
    state, nbr_in, dest_in, src_in, blk_in, wts_in, self_in, edge_in, vert_in,
    out,
    xv, nx, hl, hr, nbr, dest, src, blk, wts, surf, selfv, edgev, vertv,
    wa, wc, vcat, mo, ml, mr, sb, rb, fb, fid, db, ob, gb, tot,
    sem_x, sem_in, sem_halo_s, sem_halo_r, sem_m_s, sem_m_r,
    sem_p1_s, sem_p1_r, sem_p2_s, sem_p2_r, sem_p3_s, sem_p3_r,
):
    blocks, fields, lev, cols = state.shape
    n_gi = n_dom // NZ
    lanes = n_gi * CAP
    ocean_g = n_grp - 1
    g = lax.axis_index("grp")
    d = lax.axis_index("dom")
    gi = d // NZ
    z = lax.rem(d, NZ)
    is_ocean = g == ocean_g
    is_relay = g == RELAY
    comp = jnp.where(is_ocean, 1, 0)
    right = (g, lax.rem(d + 1, n_dom))
    left = (g, lax.rem(d + n_dom - 1, n_dom))

    per = blocks // CHUNKS
    loads_x = [
        pltpu.make_async_copy(
            state.at[pl.ds(i * per, per)], xv.at[pl.ds(i * per, per)], sem_x.at[i]
        )
        for i in range(CHUNKS)
    ]
    top = pl.multiple_of(jnp.where(is_ocean, 0, lev - 8), 8)
    pairs = [
        (nbr_in, nbr), (dest_in, dest), (src_in, src), (blk_in, blk), (wts_in, wts),
        (state.at[:, 0, pl.ds(top, 8), :], surf),
        (self_in.at[comp], selfv), (edge_in.at[comp], edgev), (vert_in.at[comp], vertv),
    ]
    loads = [pltpu.make_async_copy(a, b, sem_in.at[i]) for i, (a, b) in enumerate(pairs)]
    for c in loads:
        c.start()
    for c in loads_x:
        c.start()

    barrier = pltpu.get_barrier_semaphore()

    def greet(gg, dd):
        pl.semaphore_signal(barrier, inc=1, device_id=(gg, dd), device_id_type=MESH)

    greet(*left)
    greet(*right)

    @pl.when(is_ocean)
    def _():
        for q in range(n_gi):
            for gg in range(ocean_g):
                greet(gg, q * NZ + z)
        for r in range(1, NZ):
            greet(ocean_g, gi * NZ + lax.rem(z + r, NZ))

    @pl.when(jnp.logical_not(is_ocean))
    def _():
        for q in range(n_gi):
            greet(ocean_g, q * NZ + z)

    @pl.when(is_relay)
    def _():
        for r in range(1, NZ):
            greet(RELAY, gi * NZ + lax.rem(z + r, NZ))
        for gg in range(ocean_g):
            if gg != RELAY:
                greet(gg, d)

    @pl.when(jnp.logical_not(jnp.logical_or(is_relay, is_ocean)))
    def _():
        greet(RELAY, d)

    greetings = jnp.where(
        is_ocean,
        2 + n_gi * ocean_g + NZ - 1,
        jnp.where(is_relay, 2 + n_gi + NZ - 1 + ocean_g - 1, 2 + n_gi + 1),
    )
    halo = []
    for f in range(fields):
        halo.append(
            pltpu.make_async_remote_copy(
                src_ref=state.at[pl.ds(blocks - RIM, RIM), f], dst_ref=hl.at[f],
                send_sem=sem_halo_s.at[0, f], recv_sem=sem_halo_r.at[0, f],
                device_id=right, device_id_type=MESH,
            )
        )
        halo.append(
            pltpu.make_async_remote_copy(
                src_ref=state.at[pl.ds(0, RIM), f], dst_ref=hr.at[f],
                send_sem=sem_halo_s.at[1, f], recv_sem=sem_halo_r.at[1, f],
                device_id=left, device_id_type=MESH,
            )
        )
    loads[0].wait()
    mo[...] = jnp.zeros_like(mo)
    for side in range(2):
        for k in range(2):
            b = k if side == 0 else blocks - 2 + k
            third = nbr[2, b]
            fourth = nbr[3, b]
            for j in range(5):
                count = jnp.where(third == b + j, 1.0, 0.0) + jnp.where(fourth == b + j, 1.0, 0.0)
                row = side * 16 + k * 5 + j
                mo[row : row + 1, :] = jnp.full((1, cols), count, F32)
    counts = [
        pltpu.make_async_remote_copy(
            src_ref=mo.at[pl.ds(16, 16)], dst_ref=ml, send_sem=sem_m_s.at[0],
            recv_sem=sem_m_r.at[0], device_id=right, device_id_type=MESH,
        ),
        pltpu.make_async_remote_copy(
            src_ref=mo.at[pl.ds(0, 16)], dst_ref=mr, send_sem=sem_m_s.at[1],
            recv_sem=sem_m_r.at[1], device_id=left, device_id_type=MESH,
        ),
    ]
    for c in loads[1:6]:
        c.wait()
    n_rows = n_dom * CAP
    key = lax.rem(dest[...], n_dom)
    code = blk[...] + jnp.where(is_ocean, blocks, 0) * (dest[...] // n_dom)
    toward = (iota((n_dom, n_rows), 0) == key).astype(BF16)
    before = (iota((n_rows, n_rows), 0) < iota((n_rows, n_rows), 1)).astype(BF16)
    rank = jnp.sum(toward.astype(F32) * dot(toward, before), axis=0, keepdims=True)
    slot = key.astype(F32) * CAP + rank
    perm = (iota((n_rows, n_rows), 0).astype(F32) == slot).astype(BF16)
    weights = pick(perm, wts[...])
    origin = (iota((blocks, n_rows), 0) == src[...]).astype(BF16)
    origin = dot_nt(perm, origin).astype(BF16)
    lane = (gi * CAP).astype(F32) + rank
    at_lane = (iota((cols, n_rows), 0).astype(F32) == lane).astype(BF16)
    key8 = (key // NZ) * 8 + lax.rem(key, NZ)
    coded = jnp.where(iota((n_gi * 8, n_rows), 0) == key8, code.astype(F32), 0.0).astype(BF16)
    targets = dot_nt(coded, at_lane)
    surface = jnp.where(is_ocean, surf[:, 0, :], surf[:, 7, :])
    values = weights * pick(origin, surface)
    sb[:, 0:ROWS, :] = values.reshape(n_gi, ROWS, cols)
    sb[:, ROWS:MSG, :] = targets.reshape(n_gi, 8, cols)
    to_grp = jnp.where(is_ocean, RELAY, ocean_g)
    my_slot = jnp.where(is_ocean, gi, g * n_gi + gi)
    first = [
        pltpu.make_async_remote_copy(
            src_ref=sb.at[q], dst_ref=rb.at[my_slot], send_sem=sem_p1_s.at[q],
            recv_sem=sem_p1_r.at[my_slot], device_id=(to_grp, q * NZ + z), device_id_type=MESH,
        )
        for q in range(n_gi)
    ]
    pl.semaphore_wait(barrier, greetings)
    for c in first + counts + halo:
        c.start()

    for c in loads[6:]:
        c.wait()
    eye = (iota((cols, cols), 0) == iota((cols, cols), 1)).astype(F32)
    a = eye + 0.5 * selfv[...]
    e = 0.5 * edgev[...]
    a2h, a2l = split(exact(a, a))
    ch, cl = split(exact(e, a) + exact(a, e))
    e2h, e2l = split(exact(e, e))
    wa[0:cols, 0:cols] = a2h
    wa[0:cols, cols : 2 * cols] = a2l
    wa[cols : 2 * cols, 0:cols] = ch
    wa[cols : 2 * cols, cols : 2 * cols] = cl
    for half in range(2):
        wc[half * cols : (half + 1) * cols, 0:cols] = e2h
        wc[half * cols : (half + 1) * cols, cols : 2 * cols] = e2l
    v2 = exact(vertv[...], vertv[...])
    v2h = v2.astype(BF16).astype(F32)
    vcat[...] = jnp.concatenate([v2h, v2h, v2 - v2h], axis=1).astype(BF16)

    def lateral(x, n1, n2):
        xh, xl = split(x)
        n1h, n1l = split(n1)
        n2h, n2l = split(n2)
        p = dot(jnp.concatenate([xh, n1h], axis=1), wa[...])
        p += dot(jnp.concatenate([xl, n1l], axis=1), wa[...])
        p += dot(jnp.concatenate([n2h, n2l], axis=1), wc[...])
        return p[:, 0:cols] + p[:, cols:]

    def vertical(v):
        hi = v.astype(BF16).astype(F32)
        return dot(vcat[...], jnp.concatenate([hi, v - hi, hi], axis=0).astype(BF16))

    def near(b):
        third_ = jnp.clip(nbr[2, b] - 2, 0, blocks - 1)
        fourth_ = jnp.clip(nbr[3, b] - 2, 0, blocks - 1)
        return xv[b - 1] + xv[b + 1] + xv[third_] + xv[fourth_]

    for c in loads_x:
        c.wait()
    for b in range(2, RIM + UNIT + 2):
        nx[b + 2] = near(b)

    def received_wait(dst, sem):
        pltpu.make_async_remote_copy(
            src_ref=dst, dst_ref=dst, send_sem=sem, recv_sem=sem,
            device_id=left, device_id_type=MESH,
        ).wait_recv()

    def dense(rows, ids, height):
        return pick((iota((height, lanes), 0) == ids).astype(BF16), rows)

    def second(make):
        return [make(r, gi * NZ + lax.rem(z + r, NZ)) for r in range(1, NZ)]

    def ocean_copy(r, dd):
        return pltpu.make_async_remote_copy(
            src_ref=db.at[lax.rem(z + r, NZ)], dst_ref=ob.at[z], send_sem=sem_p2_s.at[r, 0],
            recv_sem=sem_p2_r.at[z, 0], device_id=(ocean_g, dd), device_id_type=MESH,
        )

    def relay_rows(r, dd):
        zz = lax.rem(z + r, NZ)
        return pltpu.make_async_remote_copy(
            src_ref=rb.at[pl.ds(0, n_gi), pl.ds(pl.multiple_of(zz * CAP, CAP), CAP)],
            dst_ref=fb.at[z], send_sem=sem_p2_s.at[r, 0],
            recv_sem=sem_p2_r.at[z, 0], device_id=(RELAY, dd), device_id_type=MESH,
        )

    def relay_ids(r, dd):
        return pltpu.make_async_remote_copy(
            src_ref=rb.at[pl.ds(0, n_gi), pl.ds(ROWS, 8)],
            dst_ref=fid.at[z], send_sem=sem_p2_s.at[r, 1],
            recv_sem=sem_p2_r.at[z, 1], device_id=(RELAY, dd), device_id_type=MESH,
        )

    def ocean_second():
        for s in range(ocean_g * n_gi):
            received_wait(rb.at[s], sem_p1_r.at[s])
        for zz in range(NZ):
            total = jnp.zeros((blocks, cols), F32)
            for gg in range(ocean_g):
                sl = slice(gg * n_gi, (gg + 1) * n_gi)
                rows = rb[sl, zz * CAP : (zz + 1) * CAP, :].reshape(lanes, cols)
                ids = jnp.sum(rb[sl, ROWS:MSG, :], axis=0)[zz : zz + 1, 0:lanes].astype(jnp.int32)
                total += dense(rows, ids, blocks)
            db[zz] = total
        for c in second(ocean_copy):
            c.start()

    def relay_second():
        for s in range(n_gi):
            received_wait(rb.at[s], sem_p1_r.at[s])
        for c in second(relay_rows) + second(relay_ids):
            c.start()

    def third(gg, slot_):
        return pltpu.make_async_remote_copy(
            src_ref=tot.at[pl.ds(gg * blocks, blocks)], dst_ref=gb,
            send_sem=sem_p3_s.at[slot_], recv_sem=sem_p3_r.at[0],
            device_id=(gg, d), device_id_type=MESH,
        )

    def thirds():
        others = [gg for gg in range(ocean_g) if gg != RELAY]
        return [third(gg, i) for i, gg in enumerate(others)]

    def relay_third():
        own_rows = rb[0:n_gi, pl.ds(pl.multiple_of(z * CAP, CAP), CAP), :]
        own_ids = rb[0:n_gi, ROWS:MSG, :]

        def add(rows, ids8):
            mine = jnp.where(iota((8, cols), 0) == z, jnp.sum(ids8, axis=0), 0.0)
            ids = jnp.sum(mine, axis=0, keepdims=True)[:, 0:lanes].astype(jnp.int32)
            return dense(rows.reshape(lanes, cols), ids, ocean_g * blocks)

        tot[...] = add(own_rows, own_ids)
        for r in range(1, NZ):
            zz = lax.rem(z + r, NZ)
            received_wait(fb.at[zz], sem_p2_r.at[zz, 0])
            received_wait(fid.at[zz], sem_p2_r.at[zz, 1])
            tot[...] += add(fb[zz], fid[zz])
        for c in thirds():
            c.start()

    def advance(xs, n1s, n2s):
        lat = lateral(*(jnp.concatenate(v, axis=0) for v in (xs, n1s, n2s)))
        res = []
        for o in range(0, lat.shape[0], 2 * lev):
            pair = jnp.concatenate([lat[o : o + lev], lat[o + lev : o + 2 * lev]], axis=1)
            both = vertical(pair)
            res += [both[:, 0:cols], both[:, cols:]]
        return res

    def second_sum(b, f=slice(None)):
        return nx[b + 1, f] + nx[b + 3, f] + nx[nbr[2, b], f] + nx[nbr[3, b], f]

    def outer(f0):
        two = slice(f0, f0 + 2)
        for c in (counts if f0 == 0 else []) + halo[2 * f0 : 2 * f0 + 4]:
            c.wait_recv()
        for side in range(2):

            def at(k):
                if side == 0:
                    return hl[two, k] if k < RIM else xv[k - RIM, two]
                return xv[blocks - RIM + k, two] if k < RIM else hr[two, k - RIM]

            for k in range(2, 6):
                if side == 0:
                    m, row = (ml, (k - 2) * 5) if k < 4 else (mo, (k - 4) * 5)
                else:
                    m, row = (mr, (k - 4) * 5) if k >= 4 else (mo, 16 + (k - 2) * 5)
                acc = at(k - 1) + at(k + 1)
                for j in range(5):
                    acc += m[row + j : row + j + 1, :] * at(k - 2 + j)
                nx[k - 2 if side == 0 else blocks - 2 + k, two] = acc
        mine = [*range(RIM), *range(blocks - RIM, blocks)]
        high = 2 * lev
        res = advance(
            [xv[b, two].reshape(high, cols) for b in mine],
            [nx[b + 2, two].reshape(high, cols) for b in mine],
            [second_sum(b, two).reshape(high, cols) for b in mine],
        )
        for u, b in enumerate(mine):
            out[b, f0] = res[2 * u]
            out[b, f0 + 1] = res[2 * u + 1]

    def step(i, carry):
        pl.when(jnp.logical_and(is_ocean, i == SECOND))(ocean_second)
        pl.when(jnp.logical_and(is_relay, i == SECOND))(relay_second)
        pl.when(i == EARLY)(lambda: outer(0))
        mine = [RIM + i * UNIT + u for u in range(UNIT)]
        high = fields * lev
        res = advance(
            [xv[b].reshape(high, cols) for b in mine],
            [nx[b + 2].reshape(high, cols) for b in mine],
            [second_sum(b).reshape(high, cols) for b in mine],
        )
        for u, b in enumerate(mine):
            for f in range(fields):
                out[b, f] = res[u * fields + f]
        for u in range(UNIT):
            later = jnp.minimum(RIM + (i + 1) * UNIT + 2 + u, blocks - 3)
            nx[later + 2] = near(later)
        return carry

    lax.fori_loop(0, (blocks - 2 * RIM) // UNIT, step, 0)
    outer(2)
    pl.when(is_relay)(relay_third)

    @pl.when(is_ocean)
    def _():
        got = db[z]
        for r in range(1, NZ):
            zz = lax.rem(z + r, NZ)
            received_wait(ob.at[zz], sem_p2_r.at[zz, 0])
            got += ob[zz]
        out[:, 0, 0, :] += got
        for c in second(ocean_copy):
            c.wait_send()

    @pl.when(is_relay)
    def _():
        out[:, 0, lev - 1, :] += tot[RELAY * blocks : (RELAY + 1) * blocks, :]
        for c in second(relay_rows) + second(relay_ids) + thirds():
            c.wait_send()

    @pl.when(jnp.logical_not(jnp.logical_or(is_relay, is_ocean)))
    def _():
        received_wait(gb, sem_p3_r.at[0])
        out[:, 0, lev - 1, :] += gb[...]

    for c in halo + counts + first:
        c.wait_send()


def per_device(
    state, neighbours, remap_dest, remap_src, remap_block, remap_weights, self_op, edge_op, vert_op
):
    n_grp = lax.axis_size("grp")
    n_dom = lax.axis_size("dom")
    blocks, fields, lev, cols = state.shape
    n_rows = remap_dest.shape[0]
    n_gi = n_dom // NZ
    dma = pltpu.SemaphoreType.DMA
    vm = pltpu.VMEM
    call = pl.pallas_call(
        functools.partial(kernel, n_grp, n_dom),
        out_shape=pltpu.VMEM(state.shape, F32),
        in_specs=[pl.BlockSpec(memory_space=pl.ANY)] * 9,
        out_specs=pl.BlockSpec(memory_space=pltpu.VMEM),
        scratch_shapes=[
            vm(state.shape, F32),
            vm((blocks + 4, fields, lev, cols), F32),
            vm((fields, RIM, lev, cols), F32),
            vm((fields, RIM, lev, cols), F32),
            pltpu.SMEM(neighbours.shape[::-1], jnp.int32),
            vm((1, n_rows), jnp.int32),
            vm((1, n_rows), jnp.int32),
            vm((1, n_rows), jnp.int32),
            vm((n_rows, cols), F32),
            vm((blocks, 8, cols), F32),
            vm((cols, cols), F32),
            vm((cols, cols), F32),
            vm((lev, lev), F32),
            vm((2 * cols, 2 * cols), BF16),
            vm((2 * cols, 2 * cols), BF16),
            vm((lev, 3 * lev), BF16),
            vm((32, cols), F32),
            vm((16, cols), F32),
            vm((16, cols), F32),
            vm((n_gi, MSG, cols), F32),
            vm(((n_grp - 1) * n_gi, MSG, cols), F32),
            vm((NZ, n_gi, CAP, cols), F32),
            vm((NZ, n_gi, 8, cols), F32),
            vm((NZ, blocks, cols), F32),
            vm((NZ, blocks, cols), F32),
            vm((blocks, cols), F32),
            vm(((n_grp - 1) * blocks, cols), F32),
            dma((CHUNKS,)),
            dma((9,)),
            dma((2, fields)),
            dma((2, fields)),
            dma((2,)),
            dma((2,)),
            dma((n_gi,)),
            dma(((n_grp - 1) * n_gi,)),
            dma((NZ, 2)),
            dma((NZ, 2)),
            dma((n_grp - 2,)),
            dma((1,)),
        ],
        compiler_params=pltpu.CompilerParams(
            collective_id=0, has_side_effects=True, vmem_limit_bytes=46 * 1024 * 1024
        ),
        name="interval",
    )
    return call(
        state,
        neighbours.T,
        remap_dest.reshape(1, n_rows),
        remap_src.reshape(1, n_rows),
        remap_block.reshape(1, n_rows),
        remap_weights,
        self_op,
        edge_op,
        vert_op,
    )


def solution(mesh):
    in_specs = (
        P(("grp", "dom"), None, None, None),
        P(("grp", "dom"), None),
        P(("grp", "dom")),
        P(("grp", "dom")),
        P(("grp", "dom")),
        P(("grp", "dom"), None),
        P(),
        P(),
        P(),
    )
    out_specs = P(("grp", "dom"), None, None, None)
    return jax.shard_map(
        per_device, mesh=mesh, in_specs=in_specs, out_specs=out_specs, check_vma=False
    )
```

```python
import functools

import jax
import jax.numpy as jnp
from jax import lax
from jax.experimental import pallas as pl
from jax.experimental.pallas import tpu as pltpu
from jax.sharding import PartitionSpec as P

MESH = pl.DeviceIdType.MESH
F32 = jnp.float32
BF16 = jnp.bfloat16
NZ = 4
CAP = 16
RIM = 4
NEAR = 0
RELAY = 1
ROWS = NZ * CAP
MSG = ROWS + 8
CHUNKS = 4
UNIT = 8
SECOND = 6
EARLY = 6


def split(v):
    hi = v.astype(BF16)
    return hi, (v - hi.astype(F32)).astype(BF16)


def dot(a, b):
    return jnp.dot(a, b, preferred_element_type=F32)


def dot_nt(a, b):
    return lax.dot_general(a, b, (((1,), (1,)), ((), ())), preferred_element_type=F32)


def exact(a, b):
    return jnp.dot(a, b, precision=lax.Precision.HIGHEST, preferred_element_type=F32)


def pick(onehot, v):
    hi, lo = split(v)
    both = dot(onehot, jnp.concatenate([hi, lo], axis=1))
    width = v.shape[1]
    return both[:, :width] + both[:, width:]


def iota(shape, dim):
    return lax.broadcasted_iota(jnp.int32, shape, dim)


def kernel(
    n_grp, n_dom,
    state, nbr_in, dest_in, src_in, blk_in, wts_in, self_in, edge_in, vert_in,
    out,
    xv, nx, hl, hr, nbr, dest, src, blk, wts, surf, selfv, edgev, vertv,
    wa, wc, vcat, mo, ml, mr, sb, rb, fb, fid, db, ob, gb, tot,
    sem_x, sem_in, sem_halo_s, sem_halo_r, sem_m_s, sem_m_r,
    sem_p1_s, sem_p1_r, sem_p2_s, sem_p2_r, sem_p3_s, sem_p3_r,
):
    blocks, fields, lev, cols = state.shape
    n_gi = n_dom // NZ
    lanes = n_gi * CAP
    ocean_g = n_grp - 1
    g = lax.axis_index("grp")
    d = lax.axis_index("dom")
    gi = d // NZ
    z = lax.rem(d, NZ)
    is_ocean = g == ocean_g
    is_relay = g == RELAY
    is_near = g == NEAR
    n_y = n_gi // 2
    y, x_hi = gi // 2, lax.rem(gi, 2)
    x_lo = g // 2
    def collector(q):
        same = lax.rem(q, 2) == x_hi
        return jnp.where(jnp.where(same, x_lo, 1 - x_lo) == 0, NEAR, ocean_g)

    def senders():
        res = []
        for gg in range(ocean_g):
            hi = jnp.where(x_lo == gg // 2, x_hi, 1 - x_hi)
            res += [(gg, (yy * 2 + hi) * NZ + z) for yy in range(n_y)]
        return res
    comp = jnp.where(is_ocean, 1, 0)
    right = (g, lax.rem(d + 1, n_dom))
    left = (g, lax.rem(d + n_dom - 1, n_dom))

    per = blocks // CHUNKS
    loads_x = [
        pltpu.make_async_copy(
            state.at[pl.ds(i * per, per)], xv.at[pl.ds(i * per, per)], sem_x.at[i]
        )
        for i in range(CHUNKS)
    ]
    top = pl.multiple_of(jnp.where(is_ocean, 0, lev - 8), 8)
    pairs = [
        (nbr_in, nbr), (dest_in, dest), (src_in, src), (blk_in, blk), (wts_in, wts),
        (state.at[:, 0, pl.ds(top, 8), :], surf),
        (self_in.at[comp], selfv), (edge_in.at[comp], edgev), (vert_in.at[comp], vertv),
    ]
    loads = [pltpu.make_async_copy(a, b, sem_in.at[i]) for i, (a, b) in enumerate(pairs)]
    for c in loads:
        c.start()
    for c in loads_x:
        c.start()

    barrier = pltpu.get_barrier_semaphore()

    def greet(gg, dd):
        pl.semaphore_signal(barrier, inc=1, device_id=(gg, dd), device_id_type=MESH)

    greet(*left)
    greet(*right)

    def greet_senders(own):
        for gg, dd in senders():
            if own and gg == NEAR:
                pl.when(dd != d)(functools.partial(greet, gg, dd))
            else:
                greet(gg, dd)

    @pl.when(is_ocean)
    def _():
        greet_senders(False)
        for q in range(n_gi):
            greet(RELAY, q * NZ + z)
        for r in range(1, NZ):
            greet(ocean_g, gi * NZ + lax.rem(z + r, NZ))
        for r in range(NZ):
            greet(NEAR, gi * NZ + r)

    @pl.when(jnp.logical_not(is_ocean))
    def _():
        for q in range(n_gi):
            pl.when(jnp.logical_not(jnp.logical_and(is_near, gi == q)))(
                functools.partial(greet, collector(q), q * NZ + z)
            )

    @pl.when(is_near)
    def _():
        greet_senders(True)
        for r in range(NZ):
            greet(ocean_g, gi * NZ + r)

    @pl.when(is_relay)
    def _():
        for q in range(n_gi):
            greet(ocean_g, q * NZ + z)
        for r in range(1, NZ):
            greet(RELAY, gi * NZ + lax.rem(z + r, NZ))
        for gg in range(ocean_g):
            if gg != RELAY:
                greet(gg, d)

    @pl.when(jnp.logical_not(jnp.logical_or(is_relay, is_ocean)))
    def _():
        greet(RELAY, d)

    n_in = ocean_g * n_y
    greetings = 2 + n_gi + jnp.where(
        is_ocean,
        n_in + NZ - 1 + NZ,
        jnp.where(is_relay, n_gi + NZ - 1 + ocean_g - 1, jnp.where(is_near, n_in - 2 + NZ + 1, 1)),
    )

    halo = []
    for f in range(fields):
        halo.append(
            pltpu.make_async_remote_copy(
                src_ref=state.at[pl.ds(blocks - RIM, RIM), f], dst_ref=hl.at[f],
                send_sem=sem_halo_s.at[0, f], recv_sem=sem_halo_r.at[0, f],
                device_id=right, device_id_type=MESH,
            )
        )
        halo.append(
            pltpu.make_async_remote_copy(
                src_ref=state.at[pl.ds(0, RIM), f], dst_ref=hr.at[f],
                send_sem=sem_halo_s.at[1, f], recv_sem=sem_halo_r.at[1, f],
                device_id=left, device_id_type=MESH,
            )
        )
    loads[0].wait()
    mo[...] = jnp.zeros_like(mo)
    for side in range(2):
        for k in range(2):
            b = k if side == 0 else blocks - 2 + k
            third = nbr[2, b]
            fourth = nbr[3, b]
            for j in range(5):
                count = jnp.where(third == b + j, 1.0, 0.0) + jnp.where(fourth == b + j, 1.0, 0.0)
                row = side * 16 + k * 5 + j
                mo[row : row + 1, :] = jnp.full((1, cols), count, F32)
    counts = [
        pltpu.make_async_remote_copy(
            src_ref=mo.at[pl.ds(16, 16)], dst_ref=ml, send_sem=sem_m_s.at[0],
            recv_sem=sem_m_r.at[0], device_id=right, device_id_type=MESH,
        ),
        pltpu.make_async_remote_copy(
            src_ref=mo.at[pl.ds(0, 16)], dst_ref=mr, send_sem=sem_m_s.at[1],
            recv_sem=sem_m_r.at[1], device_id=left, device_id_type=MESH,
        ),
    ]
    for c in loads[1:6]:
        c.wait()
    n_rows = n_dom * CAP
    key = lax.rem(dest[...], n_dom)
    code = blk[...] + jnp.where(is_ocean, blocks, 0) * (dest[...] // n_dom)
    toward = (iota((n_dom, n_rows), 0) == key).astype(BF16)
    before = (iota((n_rows, n_rows), 0) < iota((n_rows, n_rows), 1)).astype(BF16)
    rank = jnp.sum(toward.astype(F32) * dot(toward, before), axis=0, keepdims=True)
    slot = key.astype(F32) * CAP + rank
    perm = (iota((n_rows, n_rows), 0).astype(F32) == slot).astype(BF16)
    weights = pick(perm, wts[...])
    origin = (iota((blocks, n_rows), 0) == src[...]).astype(BF16)
    origin = dot_nt(perm, origin).astype(BF16)
    my_slot = jnp.where(is_ocean, gi, g * n_y + y)
    lane = (lax.rem(my_slot, n_gi) * CAP).astype(F32) + rank
    at_lane = (iota((cols, n_rows), 0).astype(F32) == lane).astype(BF16)
    key8 = (key // NZ) * 8 + lax.rem(key, NZ)
    coded = jnp.where(iota((n_gi * 8, n_rows), 0) == key8, code.astype(F32), 0.0).astype(BF16)
    targets = dot_nt(coded, at_lane)
    surface = jnp.where(is_ocean, surf[:, 0, :], surf[:, 7, :])
    values = weights * pick(origin, surface)
    sb[:, 0:ROWS, :] = values.reshape(n_gi, ROWS, cols)
    sb[:, ROWS:MSG, :] = targets.reshape(n_gi, 8, cols)
    def first(q):
        to_grp = jnp.where(is_ocean, RELAY, collector(q))
        return pltpu.make_async_remote_copy(
            src_ref=sb.at[q], dst_ref=rb.at[my_slot], send_sem=sem_p1_s.at[q],
            recv_sem=sem_p1_r.at[my_slot], device_id=(to_grp, q * NZ + z), device_id_type=MESH,
        )

    def own_first(q):
        return pltpu.make_async_copy(sb.at[q], rb.at[my_slot], sem_p1_r.at[my_slot])

    def is_own(q):
        return jnp.logical_and(is_near, gi == q)

    pl.semaphore_wait(barrier, greetings)
    for q in range(n_gi):
        pl.when(is_own(q))(lambda q=q: own_first(q).start())
        pl.when(jnp.logical_not(is_own(q)))(lambda q=q: first(q).start())
    for c in counts + halo:
        c.start()

    for c in loads[6:]:
        c.wait()
    eye = (iota((cols, cols), 0) == iota((cols, cols), 1)).astype(F32)
    a = eye + 0.5 * selfv[...]
    e = 0.5 * edgev[...]
    a2h, a2l = split(exact(a, a))
    ch, cl = split(exact(e, a) + exact(a, e))
    e2h, e2l = split(exact(e, e))
    wa[0:cols, 0:cols] = a2h
    wa[0:cols, cols : 2 * cols] = a2l
    wa[cols : 2 * cols, 0:cols] = ch
    wa[cols : 2 * cols, cols : 2 * cols] = cl
    for half in range(2):
        wc[half * cols : (half + 1) * cols, 0:cols] = e2h
        wc[half * cols : (half + 1) * cols, cols : 2 * cols] = e2l
    v2 = exact(vertv[...], vertv[...])
    v2h = v2.astype(BF16).astype(F32)
    vcat[...] = jnp.concatenate([v2h, v2h, v2 - v2h], axis=1).astype(BF16)

    def lateral(x, n1, n2):
        xh, xl = split(x)
        n1h, n1l = split(n1)
        n2h, n2l = split(n2)
        p = dot(jnp.concatenate([xh, n1h], axis=1), wa[...])
        p += dot(jnp.concatenate([xl, n1l], axis=1), wa[...])
        p += dot(jnp.concatenate([n2h, n2l], axis=1), wc[...])
        return p[:, 0:cols] + p[:, cols:]

    def vertical(v):
        hi = v.astype(BF16).astype(F32)
        return dot(vcat[...], jnp.concatenate([hi, v - hi, hi], axis=0).astype(BF16))

    def near(b):
        third_ = jnp.clip(nbr[2, b] - 2, 0, blocks - 1)
        fourth_ = jnp.clip(nbr[3, b] - 2, 0, blocks - 1)
        return xv[b - 1] + xv[b + 1] + xv[third_] + xv[fourth_]

    for c in loads_x:
        c.wait()
    for b in range(2, RIM + UNIT + 2):
        nx[b + 2] = near(b)

    def received_wait(dst, sem):
        pltpu.make_async_remote_copy(
            src_ref=dst, dst_ref=dst, send_sem=sem, recv_sem=sem,
            device_id=left, device_id_type=MESH,
        ).wait_recv()

    def dense(rows, ids, height):
        return pick((iota((height, ids.shape[1]), 0) == ids).astype(BF16), rows)

    def second(make):
        return [make(r, gi * NZ + lax.rem(z + r, NZ)) for r in range(1, NZ)]

    def ocean_copy(r, dd):
        return pltpu.make_async_remote_copy(
            src_ref=db.at[lax.rem(z + r, NZ)], dst_ref=ob.at[NZ + z], send_sem=sem_p2_s.at[r, 0],
            recv_sem=sem_p2_r.at[NZ + z, 0], device_id=(ocean_g, dd), device_id_type=MESH,
        )

    def near_copies():
        return [
            pltpu.make_async_remote_copy(
                src_ref=db.at[r], dst_ref=ob.at[z], send_sem=sem_p2_s.at[r, 0],
                recv_sem=sem_p2_r.at[z, 0], device_id=(ocean_g, gi * NZ + r), device_id_type=MESH,
            )
            for r in range(NZ)
        ]

    def relay_rows(r, dd):
        zz = lax.rem(z + r, NZ)
        return pltpu.make_async_remote_copy(
            src_ref=rb.at[pl.ds(0, n_gi), pl.ds(pl.multiple_of(zz * CAP, CAP), CAP)],
            dst_ref=fb.at[z], send_sem=sem_p2_s.at[r, 0],
            recv_sem=sem_p2_r.at[z, 0], device_id=(RELAY, dd), device_id_type=MESH,
        )

    def relay_ids(r, dd):
        return pltpu.make_async_remote_copy(
            src_ref=rb.at[pl.ds(0, n_gi), pl.ds(ROWS, 8)],
            dst_ref=fid.at[z], send_sem=sem_p2_s.at[r, 1],
            recv_sem=sem_p2_r.at[z, 1], device_id=(RELAY, dd), device_id_type=MESH,
        )

    def collect():
        for s in range(n_in):
            received_wait(rb.at[s], sem_p1_r.at[s])
        for zz in range(NZ):
            total = jnp.zeros((blocks, cols), F32)
            for lo, hi in ((0, n_gi), (n_gi, n_in)):
                width = (hi - lo) * CAP
                rows = rb[lo:hi, zz * CAP : (zz + 1) * CAP, :].reshape(width, cols)
                ids = jnp.sum(rb[lo:hi, ROWS:MSG, :], axis=0)[zz : zz + 1, 0:width]
                total += dense(rows, ids.astype(jnp.int32), blocks)
            db[zz] = total

        @pl.when(is_ocean)
        def _():
            for c in second(ocean_copy):
                c.start()

        @pl.when(is_near)
        def _():
            for c in near_copies():
                c.start()

    def relay_second():
        for s in range(n_gi):
            received_wait(rb.at[s], sem_p1_r.at[s])
        for c in second(relay_rows) + second(relay_ids):
            c.start()

    def third(gg, slot_):
        return pltpu.make_async_remote_copy(
            src_ref=tot.at[pl.ds(gg * blocks, blocks)], dst_ref=gb,
            send_sem=sem_p3_s.at[slot_], recv_sem=sem_p3_r.at[0],
            device_id=(gg, d), device_id_type=MESH,
        )

    def thirds():
        others = [gg for gg in range(ocean_g) if gg != RELAY]
        return [third(gg, i) for i, gg in enumerate(others)]

    def relay_third():
        own_rows = rb[0:n_gi, pl.ds(pl.multiple_of(z * CAP, CAP), CAP), :]
        own_ids = rb[0:n_gi, ROWS:MSG, :]

        def add(rows, ids8):
            mine = jnp.where(iota((8, cols), 0) == z, jnp.sum(ids8, axis=0), 0.0)
            ids = jnp.sum(mine, axis=0, keepdims=True)[:, 0:lanes].astype(jnp.int32)
            return dense(rows.reshape(lanes, cols), ids, ocean_g * blocks)

        tot[...] = add(own_rows, own_ids)
        for r in range(1, NZ):
            zz = lax.rem(z + r, NZ)
            received_wait(fb.at[zz], sem_p2_r.at[zz, 0])
            received_wait(fid.at[zz], sem_p2_r.at[zz, 1])
            tot[...] += add(fb[zz], fid[zz])
        for c in thirds():
            c.start()

    def advance(xs, n1s, n2s):
        lat = lateral(*(jnp.concatenate(v, axis=0) for v in (xs, n1s, n2s)))
        res = []
        for o in range(0, lat.shape[0], 2 * lev):
            pair = jnp.concatenate([lat[o : o + lev], lat[o + lev : o + 2 * lev]], axis=1)
            both = vertical(pair)
            res += [both[:, 0:cols], both[:, cols:]]
        return res

    def second_sum(b, f=slice(None)):
        return nx[b + 1, f] + nx[b + 3, f] + nx[nbr[2, b], f] + nx[nbr[3, b], f]

    def outer(f0):
        two = slice(f0, f0 + 2)
        for c in (counts if f0 == 0 else []) + halo[2 * f0 : 2 * f0 + 4]:
            c.wait_recv()
        for side in range(2):

            def at(k):
                if side == 0:
                    return hl[two, k] if k < RIM else xv[k - RIM, two]
                return xv[blocks - RIM + k, two] if k < RIM else hr[two, k - RIM]

            for k in range(2, 6):
                if side == 0:
                    m, row = (ml, (k - 2) * 5) if k < 4 else (mo, (k - 4) * 5)
                else:
                    m, row = (mr, (k - 4) * 5) if k >= 4 else (mo, 16 + (k - 2) * 5)
                acc = at(k - 1) + at(k + 1)
                for j in range(5):
                    acc += m[row + j : row + j + 1, :] * at(k - 2 + j)
                nx[k - 2 if side == 0 else blocks - 2 + k, two] = acc
        mine = [*range(RIM), *range(blocks - RIM, blocks)]
        high = 2 * lev
        res = advance(
            [xv[b, two].reshape(high, cols) for b in mine],
            [nx[b + 2, two].reshape(high, cols) for b in mine],
            [second_sum(b, two).reshape(high, cols) for b in mine],
        )
        for u, b in enumerate(mine):
            out[b, f0] = res[2 * u]
            out[b, f0 + 1] = res[2 * u + 1]

    def step(i, carry):
        pl.when(jnp.logical_and(jnp.logical_or(is_ocean, is_near), i == SECOND))(collect)
        pl.when(jnp.logical_and(is_relay, i == SECOND))(relay_second)
        pl.when(i == EARLY)(lambda: outer(0))
        mine = [RIM + i * UNIT + u for u in range(UNIT)]
        high = fields * lev
        res = advance(
            [xv[b].reshape(high, cols) for b in mine],
            [nx[b + 2].reshape(high, cols) for b in mine],
            [second_sum(b).reshape(high, cols) for b in mine],
        )
        for u, b in enumerate(mine):
            for f in range(fields):
                out[b, f] = res[u * fields + f]
        for u in range(UNIT):
            later = jnp.minimum(RIM + (i + 1) * UNIT + 2 + u, blocks - 3)
            nx[later + 2] = near(later)
        return carry

    lax.fori_loop(0, (blocks - 2 * RIM) // UNIT, step, 0)
    outer(2)
    pl.when(is_relay)(relay_third)

    @pl.when(is_ocean)
    def _():
        got = db[z]
        for r in range(1, NZ):
            zz = lax.rem(z + r, NZ)
            received_wait(ob.at[NZ + zz], sem_p2_r.at[NZ + zz, 0])
            got += ob[NZ + zz]
        for r in range(NZ):
            received_wait(ob.at[r], sem_p2_r.at[r, 0])
            got += ob[r]
        out[:, 0, 0, :] += got
        for c in second(ocean_copy):
            c.wait_send()

    @pl.when(is_relay)
    def _():
        out[:, 0, lev - 1, :] += tot[RELAY * blocks : (RELAY + 1) * blocks, :]
        for c in second(relay_rows) + second(relay_ids) + thirds():
            c.wait_send()

    @pl.when(jnp.logical_not(jnp.logical_or(is_relay, is_ocean)))
    def _():
        received_wait(gb, sem_p3_r.at[0])
        out[:, 0, lev - 1, :] += gb[...]

    @pl.when(is_near)
    def _():
        for c in near_copies():
            c.wait_send()

    for q in range(n_gi):
        pl.when(jnp.logical_not(is_own(q)))(lambda q=q: first(q).wait_send())
    for c in halo + counts:
        c.wait_send()


def per_device(
    state, neighbours, remap_dest, remap_src, remap_block, remap_weights, self_op, edge_op, vert_op
):
    n_grp = lax.axis_size("grp")
    n_dom = lax.axis_size("dom")
    blocks, fields, lev, cols = state.shape
    n_rows = remap_dest.shape[0]
    n_gi = n_dom // NZ
    dma = pltpu.SemaphoreType.DMA
    vm = pltpu.VMEM
    call = pl.pallas_call(
        functools.partial(kernel, n_grp, n_dom),
        out_shape=pltpu.VMEM(state.shape, F32),
        in_specs=[pl.BlockSpec(memory_space=pl.ANY)] * 9,
        out_specs=pl.BlockSpec(memory_space=pltpu.VMEM),
        scratch_shapes=[
            vm(state.shape, F32),
            vm((blocks + 4, fields, lev, cols), F32),
            vm((fields, RIM, lev, cols), F32),
            vm((fields, RIM, lev, cols), F32),
            pltpu.SMEM(neighbours.shape[::-1], jnp.int32),
            vm((1, n_rows), jnp.int32),
            vm((1, n_rows), jnp.int32),
            vm((1, n_rows), jnp.int32),
            vm((n_rows, cols), F32),
            vm((blocks, 8, cols), F32),
            vm((cols, cols), F32),
            vm((cols, cols), F32),
            vm((lev, lev), F32),
            vm((2 * cols, 2 * cols), BF16),
            vm((2 * cols, 2 * cols), BF16),
            vm((lev, 3 * lev), BF16),
            vm((32, cols), F32),
            vm((16, cols), F32),
            vm((16, cols), F32),
            vm((n_gi, MSG, cols), F32),
            vm(((n_grp - 1) * n_gi // 2, MSG, cols), F32),
            vm((NZ, n_gi, CAP, cols), F32),
            vm((NZ, n_gi, 8, cols), F32),
            vm((NZ, blocks, cols), F32),
            vm((2 * NZ, blocks, cols), F32),
            vm((blocks, cols), F32),
            vm(((n_grp - 1) * blocks, cols), F32),
            dma((CHUNKS,)),
            dma((9,)),
            dma((2, fields)),
            dma((2, fields)),
            dma((2,)),
            dma((2,)),
            dma((n_gi,)),
            dma(((n_grp - 1) * n_gi // 2,)),
            dma((NZ, 2)),
            dma((2 * NZ, 2)),
            dma((n_grp - 2,)),
            dma((1,)),
        ],
        compiler_params=pltpu.CompilerParams(
            collective_id=0, has_side_effects=True, vmem_limit_bytes=46 * 1024 * 1024
        ),
        name="interval",
    )
    return call(
        state,
        neighbours.T,
        remap_dest.reshape(1, n_rows),
        remap_src.reshape(1, n_rows),
        remap_block.reshape(1, n_rows),
        remap_weights,
        self_op,
        edge_op,
        vert_op,
    )


def solution(mesh):
    in_specs = (
        P(("grp", "dom"), None, None, None),
        P(("grp", "dom"), None),
        P(("grp", "dom")),
        P(("grp", "dom")),
        P(("grp", "dom")),
        P(("grp", "dom"), None),
        P(),
        P(),
        P(),
    )
    out_specs = P(("grp", "dom"), None, None, None)
    return jax.shard_map(
        per_device, mesh=mesh, in_specs=in_specs, out_specs=out_specs, check_vma=False
    )
```

```python
import functools

import jax
import jax.numpy as jnp
from jax import lax
from jax.experimental import pallas as pl
from jax.experimental.pallas import tpu as pltpu
from jax.sharding import PartitionSpec as P

MESH = pl.DeviceIdType.MESH
F32 = jnp.float32
BF16 = jnp.bfloat16
NZ = 4
CAP = 16
RIM = 4
NEAR = 0
RELAY = 1
ROWS = NZ * CAP
MSG = ROWS + 8
CHUNKS = 4
UNIT = 8
SECOND = 6
EARLY = 6


def split(v):
    hi = v.astype(BF16)
    return hi, (v - hi.astype(F32)).astype(BF16)


def dot(a, b):
    return jnp.dot(a, b, preferred_element_type=F32)


def dot_nt(a, b):
    return lax.dot_general(a, b, (((1,), (1,)), ((), ())), preferred_element_type=F32)


def exact(a, b):
    return jnp.dot(a, b, precision=lax.Precision.HIGHEST, preferred_element_type=F32)


def pick(onehot, v):
    hi, lo = split(v)
    both = dot(onehot, jnp.concatenate([hi, lo], axis=1))
    width = v.shape[1]
    return both[:, :width] + both[:, width:]


def iota(shape, dim):
    return lax.broadcasted_iota(jnp.int32, shape, dim)


def kernel(
    n_grp, n_dom,
    state, nbr_in, dest_in, src_in, blk_in, wts_in, self_in, edge_in, vert_in,
    out,
    xv, nx, hl, hr, nbr, dest, src, blk, wts, surf, selfv, edgev, vertv,
    wa, wc, vcat, mo, ml, mr, sb, rb, fb, fid, db, ob, gb, tot,
    sem_x, sem_in, sem_halo_s, sem_halo_r, sem_m_s, sem_m_r,
    sem_p1_s, sem_p1_r, sem_p2_s, sem_p2_r, sem_p3_s, sem_p3_r,
):
    blocks, fields, lev, cols = state.shape
    n_gi = n_dom // NZ
    lanes = n_gi * CAP
    ocean_g = n_grp - 1
    g = lax.axis_index("grp")
    d = lax.axis_index("dom")
    gi = d // NZ
    z = lax.rem(d, NZ)
    is_ocean = g == ocean_g
    is_relay = g == RELAY
    is_near = g == NEAR
    n_y = n_gi // 2
    y, x_hi = gi // 2, lax.rem(gi, 2)
    x_lo = g // 2
    def collector(q):
        same = lax.rem(q, 2) == x_hi
        return jnp.where(jnp.where(same, x_lo, 1 - x_lo) == 0, NEAR, ocean_g)

    def senders():
        res = []
        for gg in range(ocean_g):
            hi = jnp.where(x_lo == gg // 2, x_hi, 1 - x_hi)
            res += [(gg, (yy * 2 + hi) * NZ + z) for yy in range(n_y)]
        return res
    comp = jnp.where(is_ocean, 1, 0)
    right = (g, lax.rem(d + 1, n_dom))
    left = (g, lax.rem(d + n_dom - 1, n_dom))

    per = blocks // CHUNKS
    loads_x = [
        pltpu.make_async_copy(
            state.at[pl.ds(i * per, per)], xv.at[pl.ds(i * per, per)], sem_x.at[i]
        )
        for i in range(CHUNKS)
    ]
    top = pl.multiple_of(jnp.where(is_ocean, 0, lev - 8), 8)
    pairs = [
        (nbr_in, nbr), (dest_in, dest), (src_in, src), (blk_in, blk), (wts_in, wts),
        (state.at[:, 0, pl.ds(top, 8), :], surf),
        (self_in.at[comp], selfv), (edge_in.at[comp], edgev), (vert_in.at[comp], vertv),
    ]
    loads = [pltpu.make_async_copy(a, b, sem_in.at[i]) for i, (a, b) in enumerate(pairs)]
    for c in loads:
        c.start()
    for c in loads_x:
        c.start()

    barrier = pltpu.get_barrier_semaphore()

    def greet(gg, dd):
        pl.semaphore_signal(barrier, inc=1, device_id=(gg, dd), device_id_type=MESH)

    greet(*left)
    greet(*right)

    def greet_senders(own):
        for gg, dd in senders():
            if own and gg == NEAR:
                pl.when(dd != d)(functools.partial(greet, gg, dd))
            else:
                greet(gg, dd)

    @pl.when(is_ocean)
    def _():
        greet_senders(False)
        for q in range(n_gi):
            greet(RELAY, q * NZ + z)
        for r in range(1, NZ):
            greet(ocean_g, gi * NZ + lax.rem(z + r, NZ))
        for r in range(NZ):
            greet(NEAR, gi * NZ + r)

    @pl.when(jnp.logical_not(is_ocean))
    def _():
        for q in range(n_gi):
            pl.when(jnp.logical_not(jnp.logical_and(is_near, gi == q)))(
                functools.partial(greet, collector(q), q * NZ + z)
            )

    @pl.when(is_near)
    def _():
        greet_senders(True)
        for r in range(NZ):
            greet(ocean_g, gi * NZ + r)

    @pl.when(is_relay)
    def _():
        for q in range(n_gi):
            greet(ocean_g, q * NZ + z)
        for r in range(1, NZ):
            greet(RELAY, gi * NZ + lax.rem(z + r, NZ))
        for gg in range(ocean_g):
            if gg != RELAY:
                greet(gg, d)

    @pl.when(jnp.logical_not(jnp.logical_or(is_relay, is_ocean)))
    def _():
        greet(RELAY, d)

    n_in = ocean_g * n_y
    greetings = 2 + n_gi + jnp.where(
        is_ocean,
        n_in + NZ - 1 + NZ,
        jnp.where(is_relay, n_gi + NZ - 1 + ocean_g - 1, jnp.where(is_near, n_in - 2 + NZ + 1, 1)),
    )

    halo = []
    for f in range(fields):
        halo.append(
            pltpu.make_async_remote_copy(
                src_ref=state.at[pl.ds(blocks - RIM, RIM), f], dst_ref=hl.at[f],
                send_sem=sem_halo_s.at[0, f], recv_sem=sem_halo_r.at[0, f],
                device_id=right, device_id_type=MESH,
            )
        )
        halo.append(
            pltpu.make_async_remote_copy(
                src_ref=state.at[pl.ds(0, RIM), f], dst_ref=hr.at[f],
                send_sem=sem_halo_s.at[1, f], recv_sem=sem_halo_r.at[1, f],
                device_id=left, device_id_type=MESH,
            )
        )
    loads[0].wait()
    mo[...] = jnp.zeros_like(mo)
    for side in range(2):
        for k in range(2):
            b = k if side == 0 else blocks - 2 + k
            third = nbr[2, b]
            fourth = nbr[3, b]
            for j in range(5):
                count = jnp.where(third == b + j, 1.0, 0.0) + jnp.where(fourth == b + j, 1.0, 0.0)
                row = side * 16 + k * 5 + j
                mo[row : row + 1, :] = jnp.full((1, cols), count, F32)
    counts = [
        pltpu.make_async_remote_copy(
            src_ref=mo.at[pl.ds(16, 16)], dst_ref=ml, send_sem=sem_m_s.at[0],
            recv_sem=sem_m_r.at[0], device_id=right, device_id_type=MESH,
        ),
        pltpu.make_async_remote_copy(
            src_ref=mo.at[pl.ds(0, 16)], dst_ref=mr, send_sem=sem_m_s.at[1],
            recv_sem=sem_m_r.at[1], device_id=left, device_id_type=MESH,
        ),
    ]
    for c in loads[1:6]:
        c.wait()
    n_rows = n_dom * CAP
    key = lax.rem(dest[...], n_dom)
    code = blk[...] + jnp.where(is_ocean, blocks, 0) * (dest[...] // n_dom)
    toward = (iota((n_dom, n_rows), 0) == key).astype(BF16)
    before = (iota((n_rows, n_rows), 0) < iota((n_rows, n_rows), 1)).astype(BF16)
    rank = jnp.sum(toward.astype(F32) * dot(toward, before), axis=0, keepdims=True)
    slot = key.astype(F32) * CAP + rank
    perm = (iota((n_rows, n_rows), 0).astype(F32) == slot).astype(BF16)
    weights = pick(perm, wts[...])
    origin = (iota((blocks, n_rows), 0) == src[...]).astype(BF16)
    origin = dot_nt(perm, origin).astype(BF16)
    my_slot = jnp.where(is_ocean, gi, g * n_y + y)
    lane = (lax.rem(my_slot, n_gi) * CAP).astype(F32) + rank
    at_lane = (iota((cols, n_rows), 0).astype(F32) == lane).astype(BF16)
    key8 = (key // NZ) * 8 + lax.rem(key, NZ)
    coded = jnp.where(iota((n_gi * 8, n_rows), 0) == key8, code.astype(F32), 0.0).astype(BF16)
    targets = dot_nt(coded, at_lane)
    surface = jnp.where(is_ocean, surf[:, 0, :], surf[:, 7, :])
    values = weights * pick(origin, surface)
    sb[:, 0:ROWS, :] = values.reshape(n_gi, ROWS, cols)
    sb[:, ROWS:MSG, :] = targets.reshape(n_gi, 8, cols)
    def first(q):
        to_grp = jnp.where(is_ocean, RELAY, collector(q))
        return pltpu.make_async_remote_copy(
            src_ref=sb.at[q], dst_ref=rb.at[my_slot], send_sem=sem_p1_s.at[q],
            recv_sem=sem_p1_r.at[my_slot], device_id=(to_grp, q * NZ + z), device_id_type=MESH,
        )

    def own_first(q):
        return pltpu.make_async_copy(sb.at[q], rb.at[my_slot], sem_p1_r.at[my_slot])

    def is_own(q):
        return jnp.logical_and(is_near, gi == q)

    pl.semaphore_wait(barrier, greetings)
    for q in range(n_gi):
        pl.when(is_own(q))(lambda q=q: own_first(q).start())
        pl.when(jnp.logical_not(is_own(q)))(lambda q=q: first(q).start())
    for c in counts + halo:
        c.start()

    for c in loads[6:]:
        c.wait()
    eye = (iota((cols, cols), 0) == iota((cols, cols), 1)).astype(F32)
    a = eye + 0.5 * selfv[...]
    e = 0.5 * edgev[...]
    a2h, a2l = split(exact(a, a))
    ch, cl = split(exact(e, a) + exact(a, e))
    e2h, e2l = split(exact(e, e))
    wa[0:cols, 0:cols] = a2h
    wa[0:cols, cols : 2 * cols] = a2l
    wa[cols : 2 * cols, 0:cols] = ch
    wa[cols : 2 * cols, cols : 2 * cols] = cl
    for half in range(2):
        wc[half * cols : (half + 1) * cols, 0:cols] = e2h
        wc[half * cols : (half + 1) * cols, cols : 2 * cols] = e2l
    v2 = exact(vertv[...], vertv[...])
    v2h = v2.astype(BF16).astype(F32)
    vcat[...] = jnp.concatenate([v2h, v2h, v2 - v2h], axis=1).astype(BF16)

    def lateral(x, n1, n2):
        xh, xl = split(x)
        n1h, n1l = split(n1)
        n2h, n2l = split(n2)
        p = dot(jnp.concatenate([xh, n1h], axis=1), wa[...])
        p += dot(jnp.concatenate([xl, n1l], axis=1), wa[...])
        p += dot(jnp.concatenate([n2h, n2l], axis=1), wc[...])
        return p[:, 0:cols] + p[:, cols:]

    def vertical(v):
        hi = v.astype(BF16).astype(F32)
        return dot(vcat[...], jnp.concatenate([hi, v - hi, hi], axis=0).astype(BF16))

    def near(b):
        third_ = jnp.clip(nbr[2, b] - 2, 0, blocks - 1)
        fourth_ = jnp.clip(nbr[3, b] - 2, 0, blocks - 1)
        return xv[b - 1] + xv[b + 1] + xv[third_] + xv[fourth_]

    for c in loads_x:
        c.wait()
    for b in range(2, RIM + UNIT + 2):
        nx[b + 2] = near(b)

    def received_wait(dst, sem):
        pltpu.make_async_remote_copy(
            src_ref=dst, dst_ref=dst, send_sem=sem, recv_sem=sem,
            device_id=left, device_id_type=MESH,
        ).wait_recv()

    def dense(rows, ids, height):
        return pick((iota((height, ids.shape[1]), 0) == ids).astype(BF16), rows)

    def second(make):
        return [make(r, gi * NZ + lax.rem(z + r, NZ)) for r in range(1, NZ)]

    def ocean_copy(r, dd):
        return pltpu.make_async_remote_copy(
            src_ref=db.at[lax.rem(z + r, NZ)], dst_ref=ob.at[NZ + z], send_sem=sem_p2_s.at[r, 0],
            recv_sem=sem_p2_r.at[NZ + z, 0], device_id=(ocean_g, dd), device_id_type=MESH,
        )

    def near_copies():
        return [
            pltpu.make_async_remote_copy(
                src_ref=db.at[r], dst_ref=ob.at[z], send_sem=sem_p2_s.at[r, 0],
                recv_sem=sem_p2_r.at[z, 0], device_id=(ocean_g, gi * NZ + r), device_id_type=MESH,
            )
            for r in range(NZ)
        ]

    def relay_rows(r, dd):
        zz = lax.rem(z + r, NZ)
        return pltpu.make_async_remote_copy(
            src_ref=rb.at[pl.ds(0, n_gi), pl.ds(pl.multiple_of(zz * CAP, CAP), CAP)],
            dst_ref=fb.at[z], send_sem=sem_p2_s.at[r, 0],
            recv_sem=sem_p2_r.at[z, 0], device_id=(RELAY, dd), device_id_type=MESH,
        )

    def relay_ids(r, dd):
        return pltpu.make_async_remote_copy(
            src_ref=rb.at[pl.ds(0, n_gi), pl.ds(ROWS, 8)],
            dst_ref=fid.at[z], send_sem=sem_p2_s.at[r, 1],
            recv_sem=sem_p2_r.at[z, 1], device_id=(RELAY, dd), device_id_type=MESH,
        )

    def collect():
        for s in range(n_in):
            received_wait(rb.at[s], sem_p1_r.at[s])
        for zz in range(NZ):
            total = jnp.zeros((blocks, cols), F32)
            for lo, hi in ((0, n_gi), (n_gi, n_in)):
                width = (hi - lo) * CAP
                rows = rb[lo:hi, zz * CAP : (zz + 1) * CAP, :].reshape(width, cols)
                ids = jnp.sum(rb[lo:hi, ROWS:MSG, :], axis=0)[zz : zz + 1, 0:width]
                total += dense(rows, ids.astype(jnp.int32), blocks)
            db[zz] = total

        @pl.when(is_ocean)
        def _():
            for c in second(ocean_copy):
                c.start()

        @pl.when(is_near)
        def _():
            for c in near_copies():
                c.start()

    def relay_second():
        for s in range(n_gi):
            received_wait(rb.at[s], sem_p1_r.at[s])
        for c in second(relay_rows) + second(relay_ids):
            c.start()

    def third(gg, slot_):
        return pltpu.make_async_remote_copy(
            src_ref=tot.at[pl.ds(gg * blocks, blocks)], dst_ref=gb,
            send_sem=sem_p3_s.at[slot_], recv_sem=sem_p3_r.at[0],
            device_id=(gg, d), device_id_type=MESH,
        )

    def thirds():
        others = [gg for gg in range(ocean_g) if gg != RELAY]
        return [third(gg, i) for i, gg in enumerate(others)]

    def relay_third():
        own_rows = rb[0:n_gi, pl.ds(pl.multiple_of(z * CAP, CAP), CAP), :]
        own_ids = rb[0:n_gi, ROWS:MSG, :]

        def add(rows, ids8):
            mine = jnp.where(iota((8, cols), 0) == z, jnp.sum(ids8, axis=0), 0.0)
            ids = jnp.sum(mine, axis=0, keepdims=True)[:, 0:lanes].astype(jnp.int32)
            return dense(rows.reshape(lanes, cols), ids, ocean_g * blocks)

        tot[...] = add(own_rows, own_ids)
        for r in range(1, NZ):
            zz = lax.rem(z + r, NZ)
            received_wait(fb.at[zz], sem_p2_r.at[zz, 0])
            received_wait(fid.at[zz], sem_p2_r.at[zz, 1])
            tot[...] += add(fb[zz], fid[zz])
        for c in thirds():
            c.start()

    def advance(xs, n1s, n2s):
        lat = lateral(*(jnp.concatenate(v, axis=0) for v in (xs, n1s, n2s)))
        res = []
        for o in range(0, lat.shape[0], 2 * lev):
            pair = jnp.concatenate([lat[o : o + lev], lat[o + lev : o + 2 * lev]], axis=1)
            both = vertical(pair)
            res += [both[:, 0:cols], both[:, cols:]]
        return res

    def second_sum(b, f=slice(None)):
        return nx[b + 1, f] + nx[b + 3, f] + nx[nbr[2, b], f] + nx[nbr[3, b], f]

    def outer(f0):
        two = slice(f0, f0 + 2)
        for c in (counts if f0 == 0 else []) + halo[2 * f0 : 2 * f0 + 4]:
            c.wait_recv()
        for side in range(2):

            def at(k):
                if side == 0:
                    return hl[two, k] if k < RIM else xv[k - RIM, two]
                return xv[blocks - RIM + k, two] if k < RIM else hr[two, k - RIM]

            for k in range(2, 6):
                if side == 0:
                    m, row = (ml, (k - 2) * 5) if k < 4 else (mo, (k - 4) * 5)
                else:
                    m, row = (mr, (k - 4) * 5) if k >= 4 else (mo, 16 + (k - 2) * 5)
                acc = at(k - 1) + at(k + 1)
                for j in range(5):
                    acc += m[row + j : row + j + 1, :] * at(k - 2 + j)
                nx[k - 2 if side == 0 else blocks - 2 + k, two] = acc
        mine = [*range(RIM), *range(blocks - RIM, blocks)]
        high = 2 * lev
        res = advance(
            [xv[b, two].reshape(high, cols) for b in mine],
            [nx[b + 2, two].reshape(high, cols) for b in mine],
            [second_sum(b, two).reshape(high, cols) for b in mine],
        )
        for u, b in enumerate(mine):
            out[b, f0] = res[2 * u]
            out[b, f0 + 1] = res[2 * u + 1]

    def step(i, carry):
        pl.when(jnp.logical_and(is_relay, i == SECOND))(relay_second)
        pl.when(i == EARLY)(lambda: outer(0))
        mine = [RIM + i * UNIT + u for u in range(UNIT)]
        high = fields * lev
        res = advance(
            [xv[b].reshape(high, cols) for b in mine],
            [nx[b + 2].reshape(high, cols) for b in mine],
            [second_sum(b).reshape(high, cols) for b in mine],
        )
        for u, b in enumerate(mine):
            for f in range(fields):
                out[b, f] = res[u * fields + f]
        for u in range(UNIT):
            later = jnp.minimum(RIM + (i + 1) * UNIT + 2 + u, blocks - 3)
            nx[later + 2] = near(later)
        return carry

    lax.fori_loop(0, (blocks - 2 * RIM) // UNIT, step, 0)
    pl.when(jnp.logical_or(is_ocean, is_near))(collect)
    outer(2)
    pl.when(is_relay)(relay_third)

    @pl.when(is_ocean)
    def _():
        got = db[z]
        for r in range(1, NZ):
            zz = lax.rem(z + r, NZ)
            received_wait(ob.at[NZ + zz], sem_p2_r.at[NZ + zz, 0])
            got += ob[NZ + zz]
        for r in range(NZ):
            received_wait(ob.at[r], sem_p2_r.at[r, 0])
            got += ob[r]
        out[:, 0, 0, :] += got
        for c in second(ocean_copy):
            c.wait_send()

    @pl.when(is_relay)
    def _():
        out[:, 0, lev - 1, :] += tot[RELAY * blocks : (RELAY + 1) * blocks, :]
        for c in second(relay_rows) + second(relay_ids) + thirds():
            c.wait_send()

    @pl.when(jnp.logical_not(jnp.logical_or(is_relay, is_ocean)))
    def _():
        received_wait(gb, sem_p3_r.at[0])
        out[:, 0, lev - 1, :] += gb[...]

    @pl.when(is_near)
    def _():
        for c in near_copies():
            c.wait_send()

    for q in range(n_gi):
        pl.when(jnp.logical_not(is_own(q)))(lambda q=q: first(q).wait_send())
    for c in halo + counts:
        c.wait_send()


def per_device(
    state, neighbours, remap_dest, remap_src, remap_block, remap_weights, self_op, edge_op, vert_op
):
    n_grp = lax.axis_size("grp")
    n_dom = lax.axis_size("dom")
    blocks, fields, lev, cols = state.shape
    n_rows = remap_dest.shape[0]
    n_gi = n_dom // NZ
    dma = pltpu.SemaphoreType.DMA
    vm = pltpu.VMEM
    call = pl.pallas_call(
        functools.partial(kernel, n_grp, n_dom),
        out_shape=pltpu.VMEM(state.shape, F32),
        in_specs=[pl.BlockSpec(memory_space=pl.ANY)] * 9,
        out_specs=pl.BlockSpec(memory_space=pltpu.VMEM),
        scratch_shapes=[
            vm(state.shape, F32),
            vm((blocks + 4, fields, lev, cols), F32),
            vm((fields, RIM, lev, cols), F32),
            vm((fields, RIM, lev, cols), F32),
            pltpu.SMEM(neighbours.shape[::-1], jnp.int32),
            vm((1, n_rows), jnp.int32),
            vm((1, n_rows), jnp.int32),
            vm((1, n_rows), jnp.int32),
            vm((n_rows, cols), F32),
            vm((blocks, 8, cols), F32),
            vm((cols, cols), F32),
            vm((cols, cols), F32),
            vm((lev, lev), F32),
            vm((2 * cols, 2 * cols), BF16),
            vm((2 * cols, 2 * cols), BF16),
            vm((lev, 3 * lev), BF16),
            vm((32, cols), F32),
            vm((16, cols), F32),
            vm((16, cols), F32),
            vm((n_gi, MSG, cols), F32),
            vm(((n_grp - 1) * n_gi // 2, MSG, cols), F32),
            vm((NZ, n_gi, CAP, cols), F32),
            vm((NZ, n_gi, 8, cols), F32),
            vm((NZ, blocks, cols), F32),
            vm((2 * NZ, blocks, cols), F32),
            vm((blocks, cols), F32),
            vm(((n_grp - 1) * blocks, cols), F32),
            dma((CHUNKS,)),
            dma((9,)),
            dma((2, fields)),
            dma((2, fields)),
            dma((2,)),
            dma((2,)),
            dma((n_gi,)),
            dma(((n_grp - 1) * n_gi // 2,)),
            dma((NZ, 2)),
            dma((2 * NZ, 2)),
            dma((n_grp - 2,)),
            dma((1,)),
        ],
        compiler_params=pltpu.CompilerParams(
            collective_id=0, has_side_effects=True, vmem_limit_bytes=46 * 1024 * 1024
        ),
        name="interval",
    )
    return call(
        state,
        neighbours.T,
        remap_dest.reshape(1, n_rows),
        remap_src.reshape(1, n_rows),
        remap_block.reshape(1, n_rows),
        remap_weights,
        self_op,
        edge_op,
        vert_op,
    )


def solution(mesh):
    in_specs = (
        P(("grp", "dom"), None, None, None),
        P(("grp", "dom"), None),
        P(("grp", "dom")),
        P(("grp", "dom")),
        P(("grp", "dom")),
        P(("grp", "dom"), None),
        P(),
        P(),
        P(),
    )
    out_specs = P(("grp", "dom"), None, None, None)
    return jax.shard_map(
        per_device, mesh=mesh, in_specs=in_specs, out_specs=out_specs, check_vma=False
    )
```
